32 devices in a mesh: blk: 8 (over z, x), tok: 4 (over y, core).
Axes of the slice: x: 2, y: 2, z: 4, core: 2. Of those that a mesh axis runs over, the one named last changes fastest.
Arguments:
- stream: bfloat16 [4096, 1664], P(('tok', 'blk'))
- queries: bfloat16 [4096, 1664], P(('tok', 'blk'))
- key_cache: bfloat16 [4096, 1664], P(('tok', 'blk'))
- value_cache: bfloat16 [4096, 1664], P(('tok', 'blk')), may hold values from -6 to 6
- segments: int32 [4096], P('tok'), may hold values from 63 to 4095, as said below
- stale_rows: int32 [384], P(('tok', 'blk')), may hold values from 0 to 4095, as said below
- owners: int32 [1024], P(('tok', 'blk')), may hold values from 0 to 3, as said below
- attn_gain: float32 [1664], replicated, may hold values from 0.1 to 1.9
- w_key: bfloat16 [1664, 1664], replicated, may hold values from -0.15625 to 0.15625
- key_bias: float32 [1664], replicated, may hold values from -3 to 3
- mlp_gain: float32 [1664], replicated, may hold values from 0.1 to 1.9
- w_fc: bfloat16 [1664, 8192], P(None, 'blk'), may hold values from -0.15625 to 0.15625
- b_fc: float32 [8192], P('blk'), may hold values from -3 to 3
- w_proj: bfloat16 [8192, 1664], P('blk'), may hold values from -0.125 to 0.125
- b_proj: float32 [1664], replicated, may hold values from -3 to 3
- merge_gain: float32 [1664], replicated, may hold values from 0.1 to 1.9
- w_merge: bfloat16 [1664, 1664], replicated, may hold values from -0.15625 to 0.15625
- b_merge: float32 [1664], replicated, may hold values from -3 to 3
Outputs:
- refreshed_keys: bfloat16 [4096, 1664], P(('tok', 'blk'))
- delivered: bfloat16 [4, 8, 128, 1664], P('tok', 'blk')
The draws below stay inside these ranges and needn't reach their ends.
Inputs may be any that keep to these rules, and one draw needn't show every extreme that they name: `segments`: A segment's id is the index of its last row, so ids never fall; each segment has 4 to 128 rows, a multiple of 4, and lies inside one aligned block of 1024 rows; each such block begins with a segment of 64 rows followed by one of exactly 128 rows. `stale_rows`: Distinct; the aligned block of 128 rows of each device holds exactly 12 of them, all inside that block and listed on that device; row 0 and the last row are always listed. `owners`: all merged tokens of one segment (the segment of row 4 m for merged token m) have the same owner.
All inputs are finite; a program needn't handle non-finite values.
Results may differ from the reference program's by a relative error of at most 0.011.
Values may be sent and summed in bfloat16 or wider, within the bound.
A program may use at most 192 MiB of HBM per device.

```python
import math
import jax
import jax.numpy as jnp
from jax import lax

D = 1664
HEADS = 16
HEAD_DIM = 104
FF = 8192
TOK_DEV = 128
TOKENS = 4096
MERGED_DEV = 32
REF_DEV = 12
N_BLK = 8
N_TOK = 4


def segment_ids(key):
    group_rows = TOKENS // N_TOK
    most_segs = group_rows // 4
    lengths = 4 * jax.random.randint(key, (N_TOK, most_segs), 1, TOK_DEV // 4 + 1)
    lengths = lengths.at[:, 0].set(TOK_DEV // 2)
    lengths = lengths.at[:, 1].set(TOK_DEV)
    bounds = jnp.cumsum(lengths, axis=1)
    places = jnp.arange(group_rows, dtype=jnp.int32)
    local_ids = jnp.sum((bounds[:, None, :] <= places[None, :, None]).astype(jnp.int32), axis=2)
    ends = jnp.minimum(jnp.take_along_axis(bounds, local_ids, axis=1), group_rows) - 1
    offsets = jnp.arange(N_TOK, dtype=jnp.int32)[:, None] * group_rows
    return (ends + offsets).reshape(TOKENS).astype(jnp.int32)


def draw_segments(key, part):
    return segment_ids(jax.random.fold_in(key, 11))


def draw_owners(key, part):
    seg_ids = segment_ids(jax.random.fold_in(key, 11))
    picks = jax.random.randint(jax.random.fold_in(key, 12), (TOKENS,), 0, 2 * N_TOK - 1)
    levels = jnp.maximum(picks - N_TOK + 1, 0)
    turned = jax.random.randint(jax.random.fold_in(key, 13), (), 0, N_TOK)
    table = (levels + turned) % N_TOK
    return table[seg_ids[::4]].astype(jnp.int32)


def draw_stale_rows(key, part):
    blocks = TOKENS // TOK_DEV
    block_keys = jax.random.split(jax.random.fold_in(key, 14), blocks)
    block_ids = jnp.arange(blocks, dtype=jnp.int32)
    targets = jnp.where(block_ids == 0, 0, jnp.where(block_ids == blocks - 1, TOK_DEV - 1, -1)).astype(jnp.int32)

    def one_block(single, target):
        order = jax.random.permutation(single, TOK_DEV).astype(jnp.int32)
        found = jnp.argmax(order == target).astype(jnp.int32)
        turn = jnp.where(target >= 0, found, 0)
        return jnp.roll(order, -turn)[:REF_DEV]
    picks = jax.vmap(one_block)(block_keys, targets)
    return (picks + block_ids[:, None] * TOK_DEV).reshape(-1).astype(jnp.int32)


def paired_fields(key):
    key_first = jax.random.fold_in(key, 21)
    key_second = jax.random.fold_in(key, 22)
    key_out = jnp.clip(jax.random.normal(key_first, (TOKENS, D), jnp.float32), -6.0, 6.0)
    query_out = jnp.clip(jax.random.normal(key_second, (TOKENS, D), jnp.float32), -6.0, 6.0)
    return (query_out, key_out)


def draw_queries(key, part):
    return paired_fields(key)[0].astype(jnp.bfloat16)


def draw_key_cache(key, part):
    return paired_fields(key)[1].astype(jnp.bfloat16)


def draw_stream(key, part):
    row_scale = jnp.exp(jax.random.uniform(jax.random.fold_in(key, 31), (TOKENS, 1), jnp.float32, 0.0, math.log(10.0)))
    col_scale = jnp.exp(jax.random.uniform(jax.random.fold_in(key, 32), (1, D), jnp.float32, 0.0, math.log(10.0)))
    base = jnp.clip(jax.random.normal(jax.random.fold_in(key, 33), (TOKENS, D), jnp.float32), -6.0, 6.0)
    return (0.3 * base * row_scale * col_scale).astype(jnp.bfloat16)


def block_levels(own_key, shape, cuts, least, largest):
    level = 1.0
    for position, blocks in cuts:
        heights = jax.random.uniform(jax.random.fold_in(jax.random.fold_in(own_key, 6), position), (blocks,), jnp.float32, least / len(cuts), largest / len(cuts))
        level = level * jnp.repeat(jnp.exp(heights), shape[position] // blocks).reshape((-1,) + (1,) * (len(shape) - 1 - position))
    return level


def bell_draw(rng, shape, width, most, cuts=(), kind=jnp.bfloat16):
    result = jax.random.normal(rng, shape, jnp.float32) * width
    if len(cuts) > 0:
        result = block_levels(rng, shape, cuts, -0.22, 0.18) * result
    return jnp.clip(result, min=-most, max=most).astype(kind)


def setup_inputs(seed: int = 0) -> dict:
    key_of = jax.random.split(jax.random.key(seed), 19)
    stream = draw_stream(jax.random.fold_in(key_of[18], 71), 0)
    queries = draw_queries(jax.random.fold_in(key_of[18], 71), 0)
    key_cache = draw_key_cache(jax.random.fold_in(key_of[18], 71), 0)
    value_cache = bell_draw(key_of[3], (TOKENS, D), 1.0, 6.0, ((0, 32),))
    segments = draw_segments(jax.random.fold_in(key_of[18], 71), 0)
    stale_rows = draw_stale_rows(jax.random.fold_in(key_of[18], 71), 0)
    owners = draw_owners(jax.random.fold_in(key_of[18], 71), 0)
    attn_gain = jnp.clip(1.0 + 0.18 * jax.random.normal(key_of[7], (D,), jnp.float32), 0.1, 1.9)
    w_key = bell_draw(key_of[8], (D, D), D ** -0.5, 0.15625)
    key_bias = bell_draw(key_of[9], (D,), 0.5, 3.0, (), jnp.float32)
    mlp_gain = jnp.clip(1.0 + 0.18 * jax.random.normal(key_of[10], (D,), jnp.float32), 0.1, 1.9)
    w_fc = bell_draw(key_of[11], (D, FF), D ** -0.5, 0.15625, ((1, 8),))
    b_fc = bell_draw(key_of[12], (FF,), 0.5, 3.0, ((0, 8),), jnp.float32)
    w_proj = bell_draw(key_of[13], (FF, D), (FF // 4) ** -0.5, 0.125, ((0, 8),))
    b_proj = bell_draw(key_of[14], (D,), 0.5, 3.0, (), jnp.float32)
    merge_gain = jnp.clip(1.0 + 0.18 * jax.random.normal(key_of[15], (D,), jnp.float32), 0.1, 1.9)
    w_merge = bell_draw(key_of[16], (D, D), D ** -0.5, 0.15625)
    b_merge = bell_draw(key_of[17], (D,), 0.5, 3.0, (), jnp.float32)
    return {"stream": stream, "queries": queries, "key_cache": key_cache, "value_cache": value_cache, "segments": segments, "stale_rows": stale_rows, "owners": owners, "attn_gain": attn_gain, "w_key": w_key, "key_bias": key_bias, "mlp_gain": mlp_gain, "w_fc": w_fc, "b_fc": b_fc, "w_proj": w_proj, "b_proj": b_proj, "merge_gain": merge_gain, "w_merge": w_merge, "b_merge": b_merge}


def layer_norm(values, gain):
    center = values - lax.optimization_barrier(jnp.mean(values, axis=-1, keepdims=True))
    spread = lax.optimization_barrier(jnp.mean(center * center, axis=-1, keepdims=True))
    return center * lax.rsqrt(spread + 1e-06) * gain

def reference(stream, queries, key_cache, value_cache, segments, stale_rows, owners, attn_gain, w_key, key_bias, mlp_gain, w_fc, b_fc, w_proj, b_proj, merge_gain, w_merge, b_merge):
    held = layer_norm(stream[stale_rows].astype(jnp.float32), attn_gain).astype(jnp.bfloat16)
    fresh_keys = (jnp.dot(held, w_key, preferred_element_type=jnp.float32) + key_bias).astype(jnp.bfloat16)
    refreshed = key_cache.at[stale_rows].set(fresh_keys)
    blocks = TOKENS // TOK_DEV
    zero_rows = jnp.zeros((TOK_DEV, D), jnp.bfloat16)
    key_padded = jnp.concatenate([zero_rows, refreshed, zero_rows], axis=0)
    value_padded = jnp.concatenate([zero_rows, value_cache, zero_rows], axis=0)
    minus_ones = jnp.full((TOK_DEV,), -1, jnp.int32)
    seg_padded = jnp.concatenate([minus_ones, segments.astype(jnp.int32), minus_ones], axis=0)
    factor = 1.0 / HEAD_DIM ** 0.5

    def one_block(index):
        first = (index * TOK_DEV).astype(jnp.int32)
        query_block = lax.dynamic_slice_in_dim(queries, first, TOK_DEV, 0).reshape(TOK_DEV, HEADS, HEAD_DIM).astype(jnp.float32)
        key_block = lax.dynamic_slice_in_dim(key_padded, first, 3 * TOK_DEV, 0).reshape(3 * TOK_DEV, HEADS, HEAD_DIM).astype(jnp.float32)
        value_block = lax.dynamic_slice_in_dim(value_padded, first, 3 * TOK_DEV, 0).reshape(3 * TOK_DEV, HEADS, HEAD_DIM).astype(jnp.float32)
        query_seg = lax.dynamic_slice_in_dim(segments.astype(jnp.int32), first, TOK_DEV, 0)
        key_seg = lax.dynamic_slice_in_dim(seg_padded, first, 3 * TOK_DEV, 0)
        scores = jnp.einsum('qhd,khd->hqk', query_block, key_block) * factor
        allowed = (query_seg[:, None] == key_seg[None, :])[None]
        scores = jnp.where(allowed, scores, -jnp.inf)
        top = lax.optimization_barrier(jnp.max(scores, axis=-1, keepdims=True))
        weights = jnp.exp(scores - top)
        probs = (weights / lax.optimization_barrier(jnp.sum(weights, axis=-1, keepdims=True))).astype(jnp.bfloat16)
        output = jnp.einsum('hqk,khd->qhd', probs.astype(jnp.float32), value_block)
        return output.reshape(TOK_DEV, D).astype(jnp.bfloat16)
    attended = lax.map(one_block, jnp.arange(blocks, dtype=jnp.int32)).reshape(TOKENS, D)
    mixed = stream.astype(jnp.float32) + attended.astype(jnp.float32)
    normed = layer_norm(mixed, mlp_gain).astype(jnp.bfloat16)
    units = jax.nn.gelu(jnp.dot(normed, w_fc, preferred_element_type=jnp.float32) + b_fc, approximate=False).astype(jnp.bfloat16)
    summed = jnp.dot(units, w_proj, preferred_element_type=jnp.float32)
    pooled = lax.optimization_barrier(jnp.mean((mixed + summed).reshape(TOKENS // 4, 4, D), axis=1)) + b_proj
    merge_in = layer_norm(pooled, merge_gain).astype(jnp.bfloat16)
    merged = (jnp.dot(merge_in, w_merge, preferred_element_type=jnp.float32) + b_merge).astype(jnp.bfloat16)
    merged_grid = merged.reshape(N_TOK, N_BLK, MERGED_DEV, D).astype(jnp.float32)
    owner_grid = owners.astype(jnp.int32).reshape(N_TOK, N_BLK, MERGED_DEV)
    owner_hot = (owner_grid[..., None] == jnp.arange(N_TOK, dtype=jnp.int32)).astype(jnp.int32)
    ranking = lax.optimization_barrier(jnp.sum(jnp.cumsum(owner_hot, axis=2) * owner_hot, axis=-1)) - 1
    picked = (owner_grid[:, :, None, None, :] == jnp.arange(N_TOK, dtype=jnp.int32)[None, None, :, None, None]) & (ranking[:, :, None, None, :] == jnp.arange(MERGED_DEV, dtype=jnp.int32)[None, None, None, :, None])
    placed = jnp.einsum('tbosm,tbmd->obtsd', picked.astype(jnp.float32), merged_grid)
    delivered = placed.astype(jnp.bfloat16).reshape(N_TOK, N_BLK, N_TOK * MERGED_DEV, D)
    return (refreshed, delivered)
```

```python
import jax
import jax.numpy as jnp
from jax import lax
from jax.sharding import PartitionSpec as P

HEADS = 16


def passed_along(block, axis, distance):
    devices = range(lax.axis_size(axis))
    route = [(i - distance, i) for i in devices if i - distance in devices]
    return lax.ppermute(block, axis, route)


def layer_norm(values, gain):
    center = values - jnp.mean(values, axis=-1, keepdims=True)
    spread = jnp.mean(center * center, axis=-1, keepdims=True)
    return center * lax.rsqrt(spread + 1e-06) * gain


def body(
    stream,
    queries,
    key_cache,
    value_cache,
    segments,
    stale_rows,
    owners,
    attn_gain,
    w_key,
    key_bias,
    mlp_gain,
    w_fc,
    b_fc,
    w_proj,
    b_proj,
    merge_gain,
    w_merge,
    b_merge,
):
    row_count = stream.shape[0]
    model_width = stream.shape[1]
    head_size = model_width // HEADS
    local_rows = stale_rows % row_count
    held = layer_norm(stream[local_rows].astype(jnp.float32), attn_gain).astype(jnp.bfloat16)
    fresh_keys = (jnp.dot(held, w_key, preferred_element_type=jnp.float32) + key_bias).astype(
        jnp.bfloat16
    )
    refreshed = key_cache.at[local_rows].set(fresh_keys)
    below = passed_along((refreshed, value_cache), "blk", 1)
    above = passed_along((refreshed, value_cache), "blk", -1)
    key_window = jnp.concatenate([below[0], refreshed, above[0]], axis=0).reshape(
        3 * row_count, HEADS, head_size
    )
    value_window = jnp.concatenate([below[1], value_cache, above[1]], axis=0).reshape(
        3 * row_count, HEADS, head_size
    )
    position = lax.axis_index("blk")
    minus_ones = jnp.full((row_count,), -1, jnp.int32)
    seg_padded = jnp.concatenate([minus_ones, segments, minus_ones], axis=0)
    key_seg = lax.dynamic_slice_in_dim(seg_padded, position * row_count, 3 * row_count, 0)
    query_seg = lax.dynamic_slice_in_dim(segments, position * row_count, row_count, 0)
    query_heads = queries.reshape(row_count, HEADS, head_size)
    scores = jnp.einsum(
        "qhd,khd->hqk", query_heads, key_window, preferred_element_type=jnp.float32
    ) * (1.0 / head_size**0.5)
    allowed = (query_seg[:, None] == key_seg[None, :])[None]
    scores = jnp.where(allowed, scores, -jnp.inf)
    top_score = jnp.max(scores, axis=-1, keepdims=True)
    weights = jnp.exp(scores - top_score)
    probs = (weights / jnp.sum(weights, axis=-1, keepdims=True)).astype(jnp.bfloat16)
    attended = jnp.einsum("hqk,khd->qhd", probs, value_window, preferred_element_type=jnp.float32)
    attended = attended.reshape(row_count, model_width).astype(jnp.bfloat16)
    mixed = stream.astype(jnp.float32) + attended.astype(jnp.float32)
    normed = layer_norm(mixed, mlp_gain).astype(jnp.bfloat16)
    group_units = jax.nn.gelu(
        jnp.dot(
            lax.all_gather(normed, "blk", axis=0, tiled=True),
            w_fc,
            preferred_element_type=jnp.float32,
        )
        + b_fc,
        approximate=False,
    ).astype(jnp.bfloat16)
    pooled_units = jnp.sum(
        group_units.astype(jnp.float32).reshape(group_units.shape[0] // 4, 4, -1), axis=1
    ).astype(jnp.bfloat16)
    summed = lax.psum_scatter(
        jnp.dot(pooled_units, w_proj, preferred_element_type=jnp.float32).astype(jnp.bfloat16),
        "blk",
        scatter_dimension=0,
        tiled=True,
    ).astype(jnp.float32)
    own = jnp.sum(mixed.reshape(row_count // 4, 4, model_width), axis=1)
    pooled = (own + summed) * 0.25 + b_proj
    merge_in = layer_norm(pooled, merge_gain).astype(jnp.bfloat16)
    merged = (jnp.dot(merge_in, w_merge, preferred_element_type=jnp.float32) + b_merge).astype(
        jnp.bfloat16
    )
    owner_count = lax.axis_size("tok")
    merged_rows = row_count // 4
    owner_hot = (owners[:, None] == jnp.arange(owner_count, dtype=jnp.int32)[None, :]).astype(
        jnp.int32
    )
    ranking = jnp.sum(jnp.cumsum(owner_hot, axis=0) * owner_hot, axis=-1) - 1
    selector = (
        owners[None, None, :] == jnp.arange(owner_count, dtype=jnp.int32)[:, None, None]
    ) & (ranking[None, None, :] == jnp.arange(merged_rows, dtype=jnp.int32)[None, :, None])
    outgoing = jnp.einsum(
        "osm,md->osd", selector.astype(jnp.bfloat16), merged, preferred_element_type=jnp.float32
    ).astype(jnp.bfloat16)
    arrived = lax.all_to_all(outgoing, "tok", split_axis=0, concat_axis=0, tiled=True)
    delivered = arrived.reshape(1, 1, owner_count * merged_rows, model_width)
    return (refreshed, delivered)


def solution(mesh):
    return jax.shard_map(
        body,
        mesh=mesh,
        in_specs=(
            P(("tok", "blk"), None),
            P(("tok", "blk"), None),
            P(("tok", "blk"), None),
            P(("tok", "blk"), None),
            P("tok"),
            P(("tok", "blk")),
            P(("tok", "blk")),
            P(),
            P(),
            P(),
            P(),
            P(None, "blk"),
            P("blk"),
            P("blk", None),
            P(),
            P(),
            P(),
            P(),
        ),
        out_specs=(P(("tok", "blk"), None), P("tok", "blk", None, None)),
        check_vma=False,
    )
```

```python
import functools

import jax
import jax.numpy as jnp
from jax import lax
from jax.experimental import pallas as pl
from jax.experimental.pallas import tpu as pltpu
from jax.sharding import PartitionSpec as P

HEADS = 16
MESH = pl.DeviceIdType.MESH


def passed_along(block, axis, distance):
    devices = range(lax.axis_size(axis))
    route = [(i - distance, i) for i in devices if i - distance in devices]
    return lax.ppermute(block, axis, route)


def layer_norm(values, gain):
    center = values - jnp.mean(values, axis=-1, keepdims=True)
    spread = jnp.mean(center * center, axis=-1, keepdims=True)
    return center * lax.rsqrt(spread + 1e-06) * gain


def pool_matrix(groups):
    rows = lax.broadcasted_iota(jnp.int32, (groups, groups * 4), 1)
    group = lax.broadcasted_iota(jnp.int32, (groups, groups * 4), 0) * 4
    inside = (rows >= group) & (rows < group + 4)
    return jnp.where(inside, 1.0, 0.0).astype(jnp.bfloat16)


def dot(a, b):
    return jnp.dot(a, b, preferred_element_type=jnp.float32)


def mlp_kernel(
    n,
    nt,
    stream_ref,
    att_ref,
    owner_row,
    owner_col,
    mlp_gain,
    b_fc,
    b_proj,
    merge_gain,
    b_merge,
    w_fc_hbm,
    w_proj_hbm,
    w_merge_hbm,
    out_ref,
    gath,
    w_fc,
    w_proj,
    w_merge,
    pooled_units,
    part,
    landed,
    total,
    outgoing,
    arrived,
    weight_sem,
    ag_recv,
    up_send,
    down_send,
    cross_send,
    rs_send,
    rs_recv,
    out_send,
    out_recv,
):
    rows = stream_ref.shape[0]
    groups = rows // 4
    width = stream_ref.shape[1]
    units = b_fc.shape[1]
    line = n // 2
    blk = lax.axis_index("blk")
    tok = lax.axis_index("tok")
    lo = lax.rem(blk, 2)
    hi = lax.div(blk, 2)
    partner = blk + 1 - 2 * lo

    loads = [
        pltpu.make_async_copy(src, dst, weight_sem.at[k])
        for k, (src, dst) in enumerate(
            ((w_fc_hbm, w_fc), (w_proj_hbm, w_proj), (w_merge_hbm, w_merge))
        )
    ]
    for load in loads:
        load.start()

    barrier = pltpu.get_barrier_semaphore()
    for k in range(1, n):
        pl.semaphore_signal(
            barrier, inc=1, device_id={"blk": lax.rem(blk + k, n)}, device_id_type=MESH
        )
    for k in range(1, nt):
        pl.semaphore_signal(
            barrier, inc=1, device_id={"tok": lax.rem(tok + k, nt)}, device_id_type=MESH
        )
    mixed = stream_ref[...].astype(jnp.float32) + att_ref[...].astype(jnp.float32)
    gath[blk] = layer_norm(mixed, mlp_gain[...]).astype(jnp.bfloat16)
    pl.semaphore_wait(barrier, n - 1 + nt - 1)

    def passed(block, target, sems):
        return pltpu.make_async_remote_copy(
            src_ref=gath.at[block],
            dst_ref=gath.at[block],
            send_sem=sems.at[block],
            recv_sem=ag_recv.at[block],
            device_id={"blk": target},
            device_id_type=MESH,
        )

    def partial_copy(block):
        return pltpu.make_async_remote_copy(
            src_ref=part.at[block],
            dst_ref=landed.at[blk],
            send_sem=rs_send.at[block],
            recv_sem=rs_recv.at[blk],
            device_id={"blk": block},
            device_id_type=MESH,
        )

    def got(block):
        passed(block, partner, cross_send).wait_recv()

    @pl.when(hi + 1 < line)
    def _():
        passed(blk, blk + 2, up_send).start()

    @pl.when(hi > 0)
    def _():
        passed(blk, blk - 2, down_send).start()

    passed(blk, partner, cross_send).start()
    loads[0].wait()
    loads[1].wait()
    pool = pool_matrix(2 * groups)
    chunk = min(units, 256)

    def work(pair):
        block_rows = gath[pl.ds(2 * pair, 2)].reshape(2 * rows, width)
        for k in range(units // chunk):
            cols = slice(k * chunk, (k + 1) * chunk)
            pre = dot(block_rows, w_fc[:, cols]) + b_fc[:, cols]
            act = (0.5 * pre * (1.0 + lax.erf(pre * 0.7071067811865476))).astype(jnp.bfloat16)
            pooled_units[:, cols] = dot(pool, act).astype(jnp.bfloat16)
        result = dot(pooled_units[...], w_proj[...]).astype(jnp.bfloat16)
        for k in range(2):
            part[2 * pair + k] = result[k * groups : (k + 1) * groups]
        for k in range(2):
            block = 2 * pair + k

            @pl.when(block != blk)
            def _(block=block):
                partial_copy(block).start()

    def step(s, carry):
        below = hi - s
        above = hi + s

        @pl.when((s < line) & (below >= 0))
        def _():
            block = 2 * below + lo
            got(block)

            @pl.when(hi + 1 < line)
            def _():
                passed(block, blk + 2, up_send).start()

            passed(block, partner, cross_send).start()

        @pl.when((s < line) & (above < line))
        def _():
            block = 2 * above + lo
            got(block)

            @pl.when(hi > 0)
            def _():
                passed(block, blk - 2, down_send).start()

            passed(block, partner, cross_send).start()

        def side(d, inner):
            pair = hi + (2 * d - 1) * (s - 1)

            @pl.when((pair >= 0) & (pair < line) & ((d == 0) | (s > 1)))
            def _():
                got(2 * pair + 1 - lo)
                work(pair)

            return inner

        return lax.fori_loop(0, 2, side, carry)

    lax.fori_loop(1, line + 1, step, 0)

    total[...] = part[blk].astype(jnp.float32)

    def collect(k, carry):
        source = lax.rem(blk + k, n)
        pltpu.make_async_remote_copy(
            src_ref=part.at[source],
            dst_ref=landed.at[source],
            send_sem=rs_send.at[source],
            recv_sem=rs_recv.at[source],
            device_id={"blk": source},
            device_id_type=MESH,
        ).wait_recv()
        total[...] += landed[source].astype(jnp.float32)
        return carry

    lax.fori_loop(1, n, collect, 0)
    pool_own = pool_matrix(groups)
    own = dot(pool_own, stream_ref[...]) + dot(pool_own, att_ref[...])
    pooled = (own + total[...]) * 0.25 + b_proj[...]
    merge_in = layer_norm(pooled, merge_gain[...]).astype(jnp.bfloat16)
    loads[2].wait()
    merged = (dot(merge_in, w_merge[...]) + b_merge[...]).astype(jnp.bfloat16)
    first = lax.broadcasted_iota(jnp.int32, (groups, groups), 0)
    second = lax.broadcasted_iota(jnp.int32, (groups, groups), 1)
    same = (owner_col[...] == owner_row[...]) & (first < second)
    ranking = jnp.sum(jnp.where(same, 1.0, 0.0), axis=0, keepdims=True).astype(jnp.int32)
    place = owner_row[...] * groups + ranking
    slots = lax.broadcasted_iota(jnp.int32, (nt * groups, groups), 0)
    selector = jnp.where(slots == place, 1.0, 0.0).astype(jnp.bfloat16)
    outgoing[...] = dot(selector, merged).astype(jnp.bfloat16).reshape(nt, groups, width)

    def delivery(owner, source):
        return pltpu.make_async_remote_copy(
            src_ref=outgoing.at[owner],
            dst_ref=arrived.at[source],
            send_sem=out_send.at[owner],
            recv_sem=out_recv.at[source],
            device_id={"tok": owner},
            device_id_type=MESH,
        )

    for k in range(1, nt):
        delivery(lax.rem(tok + k, nt), tok).start()
    out_ref[tok] = outgoing[tok]

    def settle(j, carry):
        block = 2 * j + lo

        @pl.when((j <= hi) & (hi + 1 < line))
        def _():
            passed(block, blk + 2, up_send).wait_send()

        @pl.when((j >= hi) & (hi > 0))
        def _():
            passed(block, blk - 2, down_send).wait_send()

        passed(block, partner, cross_send).wait_send()
        return carry

    lax.fori_loop(0, line, settle, 0)

    def settle_partial(k, carry):
        partial_copy(lax.rem(blk + k, n)).wait_send()
        return carry

    lax.fori_loop(1, n, settle_partial, 0)
    for k in range(1, nt):
        other = lax.rem(tok + k, nt)
        delivery(other, other).wait_recv()
        out_ref[other] = arrived[other]
    for k in range(1, nt):
        delivery(lax.rem(tok + k, nt), tok).wait_send()


def mlp_merge(
    stream, attended, owners, mlp_gain, b_fc, b_proj, merge_gain, b_merge, w_fc, w_proj, w_merge
):
    n, nt = lax.axis_size("blk"), lax.axis_size("tok")
    rows, width = stream.shape
    groups = rows // 4
    units = w_fc.shape[1]
    vmem = pl.BlockSpec(memory_space=pltpu.VMEM)
    hbm = pl.BlockSpec(memory_space=pl.ANY)
    return pl.pallas_call(
        functools.partial(mlp_kernel, n, nt),
        out_shape=jax.ShapeDtypeStruct((nt, groups, width), jnp.bfloat16),
        in_specs=[vmem] * 9 + [hbm] * 3,
        out_specs=vmem,
        scratch_shapes=[
            pltpu.VMEM((n, rows, width), jnp.bfloat16),
            pltpu.VMEM(w_fc.shape, jnp.bfloat16),
            pltpu.VMEM(w_proj.shape, jnp.bfloat16),
            pltpu.VMEM(w_merge.shape, jnp.bfloat16),
            pltpu.VMEM((2 * groups, units), jnp.bfloat16),
            pltpu.VMEM((n, groups, width), jnp.bfloat16),
            pltpu.VMEM((n, groups, width), jnp.bfloat16),
            pltpu.VMEM((groups, width), jnp.float32),
            pltpu.VMEM((nt, groups, width), jnp.bfloat16),
            pltpu.VMEM((nt, groups, width), jnp.bfloat16),
            pltpu.SemaphoreType.DMA((3,)),
            pltpu.SemaphoreType.DMA((n,)),
            pltpu.SemaphoreType.DMA((n,)),
            pltpu.SemaphoreType.DMA((n,)),
            pltpu.SemaphoreType.DMA((n,)),
            pltpu.SemaphoreType.DMA((n,)),
            pltpu.SemaphoreType.DMA((n,)),
            pltpu.SemaphoreType.DMA((nt,)),
            pltpu.SemaphoreType.DMA((nt,)),
        ],
        compiler_params=pltpu.CompilerParams(
            collective_id=1, has_side_effects=True, vmem_limit_bytes=56 * 1024 * 1024
        ),
    )(
        stream,
        attended,
        owners.reshape(1, groups),
        owners.reshape(groups, 1),
        mlp_gain.reshape(1, width),
        b_fc.reshape(1, units),
        b_proj.reshape(1, width),
        merge_gain.reshape(1, width),
        b_merge.reshape(1, width),
        w_fc,
        w_proj,
        w_merge,
    )


def body(
    stream,
    queries,
    key_cache,
    value_cache,
    segments,
    stale_rows,
    owners,
    attn_gain,
    w_key,
    key_bias,
    mlp_gain,
    w_fc,
    b_fc,
    w_proj,
    b_proj,
    merge_gain,
    w_merge,
    b_merge,
):
    row_count = stream.shape[0]
    model_width = stream.shape[1]
    head_size = model_width // HEADS
    local_rows = stale_rows % row_count
    held = layer_norm(stream[local_rows].astype(jnp.float32), attn_gain).astype(jnp.bfloat16)
    fresh_keys = (jnp.dot(held, w_key, preferred_element_type=jnp.float32) + key_bias).astype(
        jnp.bfloat16
    )
    refreshed = key_cache.at[local_rows].set(fresh_keys)
    below = passed_along((refreshed, value_cache), "blk", 1)
    above = passed_along((refreshed, value_cache), "blk", -1)
    key_window = jnp.concatenate([below[0], refreshed, above[0]], axis=0).reshape(
        3 * row_count, HEADS, head_size
    )
    value_window = jnp.concatenate([below[1], value_cache, above[1]], axis=0).reshape(
        3 * row_count, HEADS, head_size
    )
    position = lax.axis_index("blk")
    minus_ones = jnp.full((row_count,), -1, jnp.int32)
    seg_padded = jnp.concatenate([minus_ones, segments, minus_ones], axis=0)
    key_seg = lax.dynamic_slice_in_dim(seg_padded, position * row_count, 3 * row_count, 0)
    query_seg = lax.dynamic_slice_in_dim(segments, position * row_count, row_count, 0)
    query_heads = queries.reshape(row_count, HEADS, head_size)
    scores = jnp.einsum(
        "qhd,khd->hqk", query_heads, key_window, preferred_element_type=jnp.float32
    ) * (1.0 / head_size**0.5)
    allowed = (query_seg[:, None] == key_seg[None, :])[None]
    scores = jnp.where(allowed, scores, -jnp.inf)
    top_score = jnp.max(scores, axis=-1, keepdims=True)
    weights = jnp.exp(scores - top_score)
    probs = (weights / jnp.sum(weights, axis=-1, keepdims=True)).astype(jnp.bfloat16)
    attended = jnp.einsum("hqk,khd->qhd", probs, value_window, preferred_element_type=jnp.float32)
    attended = attended.reshape(row_count, model_width).astype(jnp.bfloat16)
    arrived = mlp_merge(
        stream, attended, owners, mlp_gain, b_fc, b_proj, merge_gain, b_merge, w_fc, w_proj, w_merge
    )
    delivered = arrived.reshape(1, 1, row_count, model_width)
    return (refreshed, delivered)


def solution(mesh):
    return jax.shard_map(
        body,
        mesh=mesh,
        in_specs=(
            P(("tok", "blk"), None),
            P(("tok", "blk"), None),
            P(("tok", "blk"), None),
            P(("tok", "blk"), None),
            P("tok"),
            P(("tok", "blk")),
            P(("tok", "blk")),
            P(),
            P(),
            P(),
            P(),
            P(None, "blk"),
            P("blk"),
            P("blk", None),
            P(),
            P(),
            P(),
            P(),
        ),
        out_specs=(P(("tok", "blk"), None), P("tok", "blk", None, None)),
        check_vma=False,
    )
```

```python
import functools

import jax
import jax.numpy as jnp
from jax import lax
from jax.experimental import pallas as pl
from jax.experimental.pallas import tpu as pltpu
from jax.sharding import PartitionSpec as P

HEADS = 16
MESH = pl.DeviceIdType.MESH


def layer_norm(values, gain):
    center = values - jnp.mean(values, axis=-1, keepdims=True)
    spread = jnp.mean(center * center, axis=-1, keepdims=True)
    return center * lax.rsqrt(spread + 1e-06) * gain


def pool_matrix(groups):
    rows = lax.broadcasted_iota(jnp.int32, (groups, groups * 4), 1)
    group = lax.broadcasted_iota(jnp.int32, (groups, groups * 4), 0) * 4
    inside = (rows >= group) & (rows < group + 4)
    return jnp.where(inside, 1.0, 0.0).astype(jnp.bfloat16)


def dot(a, b):
    return jnp.dot(a, b, preferred_element_type=jnp.float32)


def mlp_kernel(
    n,
    nt,
    stream_ref,
    query_ref,
    key_ref,
    value_ref,
    key_seg,
    query_seg,
    stale_row,
    stale_col,
    attn_gain,
    key_bias,
    owner_row,
    owner_col,
    mlp_gain,
    b_fc,
    b_proj,
    merge_gain,
    b_merge,
    w_key_hbm,
    w_fc_hbm,
    w_proj_hbm,
    w_merge_hbm,
    refreshed_ref,
    out_ref,
    keys,
    values,
    fresh,
    stale_near,
    probs,
    attended,
    att_ref,
    gath,
    w_key,
    w_fc,
    w_proj,
    w_merge,
    pooled_units,
    part,
    landed,
    total,
    outgoing,
    arrived,
    weight_sem,
    halo_send,
    halo_recv,
    ag_recv,
    up_send,
    down_send,
    cross_send,
    rs_send,
    rs_recv,
    out_send,
    out_recv,
):
    rows = stream_ref.shape[0]
    groups = rows // 4
    width = stream_ref.shape[1]
    units = b_fc.shape[1]
    line = n // 2
    blk = lax.axis_index("blk")
    tok = lax.axis_index("tok")
    lo = lax.rem(blk, 2)
    hi = lax.div(blk, 2)
    partner = blk + 1 - 2 * lo

    loads = [
        pltpu.make_async_copy(src, dst, weight_sem.at[k])
        for k, (src, dst) in enumerate(
            (
                (w_key_hbm, w_key),
                (w_fc_hbm, w_fc),
                (w_proj_hbm, w_proj),
                (w_merge_hbm, w_merge),
            )
        )
    ]
    for load in loads:
        load.start()

    barrier = pltpu.get_barrier_semaphore()
    for k in range(1, n):
        pl.semaphore_signal(
            barrier, inc=1, device_id={"blk": lax.rem(blk + k, n)}, device_id_type=MESH
        )
    for k in range(1, nt):
        pl.semaphore_signal(
            barrier, inc=1, device_id={"tok": lax.rem(tok + k, nt)}, device_id_type=MESH
        )
    head_size = width // HEADS
    has_below = blk > 0
    has_above = blk + 1 < n

    def halo_copy(kind, src, dst, side):
        target = blk + 1 if side == 0 else blk - 1
        return pltpu.make_async_remote_copy(
            src_ref=src,
            dst_ref=dst,
            send_sem=halo_send.at[kind, side],
            recv_sem=halo_recv.at[kind, side],
            device_id={"blk": target},
            device_id_type=MESH,
        )

    def halo(side, kind):
        src, dst = (
            (key_ref, keys.at[2 * side]),
            (stale_row, stale_near.at[side]),
            (fresh.at[2], fresh.at[side]),
            (value_ref, values.at[2 * side]),
        )[kind]
        return halo_copy(kind, src, dst, side)

    def for_sides(kinds, what, sending):
        for side in range(2):
            there = has_above if (side == 0) == sending else has_below

            @pl.when(there)
            def _(side=side):
                for kind in kinds:
                    getattr(halo(side, kind), what)()

    pl.semaphore_wait(barrier, n - 1 + nt - 1)
    for_sides((0, 1), "start", True)

    slot_count = stale_col.shape[0]
    rows_of_slot = lax.broadcasted_iota(jnp.int32, (slot_count, rows), 1)
    pick = jnp.where(rows_of_slot == stale_col[...], 1.0, 0.0).astype(jnp.bfloat16)
    held = layer_norm(dot(pick, stream_ref[...]), attn_gain[...]).astype(jnp.bfloat16)
    loads[0].wait()
    fresh[2] = (dot(held, w_key[...]) + key_bias[...]).astype(jnp.bfloat16)
    for_sides((2, 3), "start", True)

    def refresh(cache, stale, new_rows):
        row_ids = lax.broadcasted_iota(jnp.int32, (rows, slot_count), 0)
        spread = jnp.where(row_ids == stale[0:1, :slot_count], 1.0, 0.0)
        hit = jnp.sum(spread, axis=1, keepdims=True) > 0.5
        return jnp.where(
            hit, dot(spread.astype(jnp.bfloat16), new_rows), cache.astype(jnp.float32)
        ).astype(jnp.bfloat16)

    keys[1] = refresh(key_ref[...], stale_row[...], fresh[2])
    refreshed_ref[...] = keys[1]
    values[1] = value_ref[...]
    for side in range(2):

        @pl.when(jnp.logical_not(has_below if side == 0 else has_above))
        def _(side=side):
            keys[2 * side] = jnp.zeros((rows, width), jnp.bfloat16)
            values[2 * side] = jnp.zeros((rows, width), jnp.bfloat16)

        @pl.when(has_below if side == 0 else has_above)
        def _(side=side):
            for kind in range(3):
                halo(side, kind).wait_recv()
            keys[2 * side] = refresh(keys[2 * side], stale_near[side], fresh[side])

    allowed = query_seg[...] == key_seg[...]

    def window(head):
        first = head * head_size // 128 * 128
        last = min(first + 256, width)
        lane = lax.broadcasted_iota(jnp.int32, (rows, last - first), 1) + first
        mine = (lane >= head * head_size) & (lane < (head + 1) * head_size)
        return slice(first, last), mine

    for head in range(HEADS):
        cols, mine = window(head)
        query = jnp.where(mine, query_ref[:, cols].astype(jnp.float32), 0.0).astype(jnp.bfloat16)
        near = keys[:, :, cols].reshape(3 * rows, cols.stop - cols.start)
        scores = lax.dot_general(
            query, near, (((1,), (1,)), ((), ())), preferred_element_type=jnp.float32
        ) * (1.0 / head_size**0.5)
        scores = jnp.where(allowed, scores, -jnp.inf)
        weights = jnp.exp(scores - jnp.max(scores, axis=-1, keepdims=True))
        probs[head] = (weights / jnp.sum(weights, axis=-1, keepdims=True)).astype(jnp.bfloat16)

    for_sides((3,), "wait_recv", False)
    attended[...] = jnp.zeros_like(attended)
    for head in range(HEADS):
        cols, mine = window(head)
        near = values[:, :, cols].reshape(3 * rows, cols.stop - cols.start)
        attended[:, cols] += jnp.where(mine, dot(probs[head], near), 0.0)
    att_ref[...] = attended[...].astype(jnp.bfloat16)
    mixed = stream_ref[...].astype(jnp.float32) + att_ref[...].astype(jnp.float32)
    gath[blk] = layer_norm(mixed, mlp_gain[...]).astype(jnp.bfloat16)

    def passed(block, target, sems):
        return pltpu.make_async_remote_copy(
            src_ref=gath.at[block],
            dst_ref=gath.at[block],
            send_sem=sems.at[block],
            recv_sem=ag_recv.at[block],
            device_id={"blk": target},
            device_id_type=MESH,
        )

    def partial_copy(block):
        return pltpu.make_async_remote_copy(
            src_ref=part.at[block],
            dst_ref=landed.at[blk],
            send_sem=rs_send.at[block],
            recv_sem=rs_recv.at[blk],
            device_id={"blk": block},
            device_id_type=MESH,
        )

    def got(block):
        passed(block, partner, cross_send).wait_recv()

    @pl.when(hi + 1 < line)
    def _():
        passed(blk, blk + 2, up_send).start()

    @pl.when(hi > 0)
    def _():
        passed(blk, blk - 2, down_send).start()

    passed(blk, partner, cross_send).start()
    loads[1].wait()
    loads[2].wait()
    pool = pool_matrix(2 * groups)
    chunk = min(units, 256)

    def work(pair):
        block_rows = gath[pl.ds(2 * pair, 2)].reshape(2 * rows, width)
        for k in range(units // chunk):
            cols = slice(k * chunk, (k + 1) * chunk)
            pre = dot(block_rows, w_fc[:, cols]) + b_fc[:, cols]
            act = (0.5 * pre * (1.0 + lax.erf(pre * 0.7071067811865476))).astype(jnp.bfloat16)
            pooled_units[:, cols] = dot(pool, act).astype(jnp.bfloat16)
        result = dot(pooled_units[...], w_proj[...]).astype(jnp.bfloat16)
        for k in range(2):
            part[2 * pair + k] = result[k * groups : (k + 1) * groups]
        for k in range(2):
            block = 2 * pair + k

            @pl.when(block != blk)
            def _(block=block):
                partial_copy(block).start()

    def step(s, carry):
        below = hi - s
        above = hi + s

        @pl.when((s < line) & (below >= 0))
        def _():
            block = 2 * below + lo
            got(block)

            @pl.when(hi + 1 < line)
            def _():
                passed(block, blk + 2, up_send).start()

            passed(block, partner, cross_send).start()

        @pl.when((s < line) & (above < line))
        def _():
            block = 2 * above + lo
            got(block)

            @pl.when(hi > 0)
            def _():
                passed(block, blk - 2, down_send).start()

            passed(block, partner, cross_send).start()

        def side(d, inner):
            pair = hi + (2 * d - 1) * (s - 1)

            @pl.when((pair >= 0) & (pair < line) & ((d == 0) | (s > 1)))
            def _():
                got(2 * pair + 1 - lo)
                work(pair)

            return inner

        return lax.fori_loop(0, 2, side, carry)

    lax.fori_loop(1, line + 1, step, 0)

    total[...] = part[blk].astype(jnp.float32)

    def collect(k, carry):
        source = lax.rem(blk + k, n)
        pltpu.make_async_remote_copy(
            src_ref=part.at[source],
            dst_ref=landed.at[source],
            send_sem=rs_send.at[source],
            recv_sem=rs_recv.at[source],
            device_id={"blk": source},
            device_id_type=MESH,
        ).wait_recv()
        total[...] += landed[source].astype(jnp.float32)
        return carry

    lax.fori_loop(1, n, collect, 0)
    pool_own = pool_matrix(groups)
    own = dot(pool_own, stream_ref[...]) + dot(pool_own, att_ref[...])
    pooled = (own + total[...]) * 0.25 + b_proj[...]
    merge_in = layer_norm(pooled, merge_gain[...]).astype(jnp.bfloat16)
    loads[3].wait()
    merged = (dot(merge_in, w_merge[...]) + b_merge[...]).astype(jnp.bfloat16)
    first = lax.broadcasted_iota(jnp.int32, (groups, groups), 0)
    second = lax.broadcasted_iota(jnp.int32, (groups, groups), 1)
    same = (owner_col[...] == owner_row[...]) & (first < second)
    ranking = jnp.sum(jnp.where(same, 1.0, 0.0), axis=0, keepdims=True).astype(jnp.int32)
    place = owner_row[...] * groups + ranking
    slots = lax.broadcasted_iota(jnp.int32, (nt * groups, groups), 0)
    selector = jnp.where(slots == place, 1.0, 0.0).astype(jnp.bfloat16)
    outgoing[...] = dot(selector, merged).astype(jnp.bfloat16).reshape(nt, groups, width)

    def delivery(owner, source):
        return pltpu.make_async_remote_copy(
            src_ref=outgoing.at[owner],
            dst_ref=arrived.at[source],
            send_sem=out_send.at[owner],
            recv_sem=out_recv.at[source],
            device_id={"tok": owner},
            device_id_type=MESH,
        )

    for k in range(1, nt):
        delivery(lax.rem(tok + k, nt), tok).start()
    out_ref[tok] = outgoing[tok]

    def settle(j, carry):
        block = 2 * j + lo

        @pl.when((j <= hi) & (hi + 1 < line))
        def _():
            passed(block, blk + 2, up_send).wait_send()

        @pl.when((j >= hi) & (hi > 0))
        def _():
            passed(block, blk - 2, down_send).wait_send()

        passed(block, partner, cross_send).wait_send()
        return carry

    lax.fori_loop(0, line, settle, 0)
    for_sides((0, 1, 2, 3), "wait_send", True)

    def settle_partial(k, carry):
        partial_copy(lax.rem(blk + k, n)).wait_send()
        return carry

    lax.fori_loop(1, n, settle_partial, 0)
    for k in range(1, nt):
        other = lax.rem(tok + k, nt)
        delivery(other, other).wait_recv()
        out_ref[other] = arrived[other]
    for k in range(1, nt):
        delivery(lax.rem(tok + k, nt), tok).wait_send()


def block_kernel(
    stream,
    queries,
    key_cache,
    value_cache,
    key_seg,
    query_seg,
    stale,
    owners,
    attn_gain,
    w_key,
    key_bias,
    mlp_gain,
    w_fc,
    b_fc,
    w_proj,
    b_proj,
    merge_gain,
    w_merge,
    b_merge,
):
    n, nt = lax.axis_size("blk"), lax.axis_size("tok")
    rows, width = stream.shape
    groups = rows // 4
    units = w_fc.shape[1]
    slot_count = -(-stale.shape[0] // 16) * 16
    stale_lanes = jnp.pad(stale, (0, 128 - stale.shape[0]), constant_values=-1)
    vmem = pl.BlockSpec(memory_space=pltpu.VMEM)
    hbm = pl.BlockSpec(memory_space=pl.ANY)
    return pl.pallas_call(
        functools.partial(mlp_kernel, n, nt),
        out_shape=(
            jax.ShapeDtypeStruct((rows, width), jnp.bfloat16),
            jax.ShapeDtypeStruct((nt, groups, width), jnp.bfloat16),
        ),
        in_specs=[vmem] * 17 + [hbm] * 4,
        out_specs=(vmem, vmem),
        scratch_shapes=[
            pltpu.VMEM((3, rows, width), jnp.bfloat16),
            pltpu.VMEM((3, rows, width), jnp.bfloat16),
            pltpu.VMEM((3, slot_count, width), jnp.bfloat16),
            pltpu.VMEM((2, 8, 128), jnp.int32),
            pltpu.VMEM((HEADS, rows, 3 * rows), jnp.bfloat16),
            pltpu.VMEM((rows, width), jnp.float32),
            pltpu.VMEM((rows, width), jnp.bfloat16),
            pltpu.VMEM((n, rows, width), jnp.bfloat16),
            pltpu.VMEM(w_key.shape, jnp.bfloat16),
            pltpu.VMEM(w_fc.shape, jnp.bfloat16),
            pltpu.VMEM(w_proj.shape, jnp.bfloat16),
            pltpu.VMEM(w_merge.shape, jnp.bfloat16),
            pltpu.VMEM((2 * groups, units), jnp.bfloat16),
            pltpu.VMEM((n, groups, width), jnp.bfloat16),
            pltpu.VMEM((n, groups, width), jnp.bfloat16),
            pltpu.VMEM((groups, width), jnp.float32),
            pltpu.VMEM((nt, groups, width), jnp.bfloat16),
            pltpu.VMEM((nt, groups, width), jnp.bfloat16),
            pltpu.SemaphoreType.DMA((4,)),
            pltpu.SemaphoreType.DMA((4, 2)),
            pltpu.SemaphoreType.DMA((4, 2)),
            pltpu.SemaphoreType.DMA((n,)),
            pltpu.SemaphoreType.DMA((n,)),
            pltpu.SemaphoreType.DMA((n,)),
            pltpu.SemaphoreType.DMA((n,)),
            pltpu.SemaphoreType.DMA((n,)),
            pltpu.SemaphoreType.DMA((n,)),
            pltpu.SemaphoreType.DMA((nt,)),
            pltpu.SemaphoreType.DMA((nt,)),
        ],
        compiler_params=pltpu.CompilerParams(
            collective_id=1, has_side_effects=True, vmem_limit_bytes=56 * 1024 * 1024
        ),
    )(
        stream,
        queries,
        key_cache,
        value_cache,
        key_seg.reshape(1, 3 * rows),
        query_seg.reshape(rows, 1),
        jnp.broadcast_to(stale_lanes[None, :], (8, 128)),
        stale_lanes[:slot_count].reshape(slot_count, 1),
        attn_gain.reshape(1, width),
        key_bias.reshape(1, width),
        owners.reshape(1, groups),
        owners.reshape(groups, 1),
        mlp_gain.reshape(1, width),
        b_fc.reshape(1, units),
        b_proj.reshape(1, width),
        merge_gain.reshape(1, width),
        b_merge.reshape(1, width),
        w_key,
        w_fc,
        w_proj,
        w_merge,
    )


def body(
    stream,
    queries,
    key_cache,
    value_cache,
    segments,
    stale_rows,
    owners,
    attn_gain,
    w_key,
    key_bias,
    mlp_gain,
    w_fc,
    b_fc,
    w_proj,
    b_proj,
    merge_gain,
    w_merge,
    b_merge,
):
    row_count = stream.shape[0]
    model_width = stream.shape[1]
    local_rows = stale_rows % row_count
    position = lax.axis_index("blk")
    minus_ones = jnp.full((row_count,), -1, jnp.int32)
    seg_padded = jnp.concatenate([minus_ones, segments, minus_ones], axis=0)
    key_seg = lax.dynamic_slice_in_dim(seg_padded, position * row_count, 3 * row_count, 0)
    query_seg = lax.dynamic_slice_in_dim(segments, position * row_count, row_count, 0)
    refreshed, arrived = block_kernel(
        stream,
        queries,
        key_cache,
        value_cache,
        key_seg,
        query_seg,
        local_rows,
        owners,
        attn_gain,
        w_key,
        key_bias,
        mlp_gain,
        w_fc,
        b_fc,
        w_proj,
        b_proj,
        merge_gain,
        w_merge,
        b_merge,
    )
    return (refreshed, arrived.reshape(1, 1, row_count, model_width))


def solution(mesh):
    return jax.shard_map(
        body,
        mesh=mesh,
        in_specs=(
            P(("tok", "blk"), None),
            P(("tok", "blk"), None),
            P(("tok", "blk"), None),
            P(("tok", "blk"), None),
            P("tok"),
            P(("tok", "blk")),
            P(("tok", "blk")),
            P(),
            P(),
            P(),
            P(),
            P(None, "blk"),
            P("blk"),
            P("blk", None),
            P(),
            P(),
            P(),
            P(),
        ),
        out_specs=(P(("tok", "blk"), None), P("tok", "blk", None, None)),
        check_vma=False,
    )
```

```python
import functools

import jax
import jax.numpy as jnp
from jax import lax
from jax.experimental import pallas as pl
from jax.experimental.pallas import tpu as pltpu
from jax.sharding import PartitionSpec as P

HEADS = 16
MESH = pl.DeviceIdType.MESH


def layer_norm(values, gain):
    center = values - jnp.mean(values, axis=-1, keepdims=True)
    spread = jnp.mean(center * center, axis=-1, keepdims=True)
    return center * lax.rsqrt(spread + 1e-06) * gain


def pool_matrix(groups):
    rows = lax.broadcasted_iota(jnp.int32, (groups, groups * 4), 1)
    group = lax.broadcasted_iota(jnp.int32, (groups, groups * 4), 0) * 4
    inside = (rows >= group) & (rows < group + 4)
    return jnp.where(inside, 1.0, 0.0).astype(jnp.bfloat16)


def column(row):
    size = row.shape[1]
    first = lax.broadcasted_iota(jnp.int32, (size, size), 0)
    second = lax.broadcasted_iota(jnp.int32, (size, size), 1)
    spread = jnp.where(first == second, row.astype(jnp.float32), 0.0)
    return jnp.sum(spread, axis=1, keepdims=True).astype(jnp.int32)


def dot(a, b):
    return jnp.dot(a, b, preferred_element_type=jnp.float32)


def mlp_kernel(
    n,
    nt,
    stream_ref,
    query_ref,
    key_ref,
    value_ref,
    index_ref,
    attn_gain_ref,
    key_bias_ref,
    mlp_gain_ref,
    b_fc_ref,
    b_proj_ref,
    merge_gain_ref,
    b_merge_ref,
    w_key_hbm,
    w_fc_hbm,
    w_proj_hbm,
    w_merge_hbm,
    refreshed_ref,
    out_ref,
    keys,
    values,
    fresh,
    stale_near,
    probs,
    attended,
    att_ref,
    gath,
    w_key,
    w_fc,
    w_proj,
    w_merge,
    pooled_units,
    part,
    landed,
    total,
    outgoing,
    arrived,
    weight_sem,
    halo_send,
    halo_recv,
    ag_recv,
    up_send,
    down_send,
    cross_send,
    rs_send,
    rs_recv,
    out_send,
    out_recv,
):
    rows = stream_ref.shape[0]
    groups = rows // 4
    width = stream_ref.shape[1]
    units = b_fc_ref.shape[0]
    line = n // 2
    attn_gain, key_bias, mlp_gain, b_fc, b_proj, merge_gain, b_merge = (
        ref[...].reshape(1, ref.shape[0])
        for ref in (
            attn_gain_ref,
            key_bias_ref,
            mlp_gain_ref,
            b_fc_ref,
            b_proj_ref,
            merge_gain_ref,
            b_merge_ref,
        )
    )
    key_seg = jnp.concatenate([index_ref[k : k + 1, :rows] for k in range(3)], axis=1)
    query_seg = column(index_ref[1:2, :rows])
    slot_count = fresh.shape[1]
    stale_col = column(index_ref[3:4, :slot_count])
    owner_row = index_ref[4:5, :groups]
    owner_col = column(owner_row)
    blk = lax.axis_index("blk")
    tok = lax.axis_index("tok")
    lo = lax.rem(blk, 2)
    hi = lax.div(blk, 2)
    partner = blk + 1 - 2 * lo

    loads = [
        pltpu.make_async_copy(src, dst, weight_sem.at[k])
        for k, (src, dst) in enumerate(
            (
                (w_key_hbm, w_key),
                (w_fc_hbm, w_fc),
                (w_proj_hbm, w_proj),
                (w_merge_hbm, w_merge),
            )
        )
    ]
    for load in loads:
        load.start()

    barrier = pltpu.get_barrier_semaphore()
    for k in range(1, n):
        pl.semaphore_signal(
            barrier, inc=1, device_id={"blk": lax.rem(blk + k, n)}, device_id_type=MESH
        )
    for k in range(1, nt):
        pl.semaphore_signal(
            barrier, inc=1, device_id={"tok": lax.rem(tok + k, nt)}, device_id_type=MESH
        )
    head_size = width // HEADS
    has_below = blk > 0
    has_above = blk + 1 < n

    def halo_copy(kind, src, dst, side):
        target = blk + 1 if side == 0 else blk - 1
        return pltpu.make_async_remote_copy(
            src_ref=src,
            dst_ref=dst,
            send_sem=halo_send.at[kind, side],
            recv_sem=halo_recv.at[kind, side],
            device_id={"blk": target},
            device_id_type=MESH,
        )

    def halo(side, kind):
        src, dst = (
            (key_ref, keys.at[2 * side]),
            (index_ref, stale_near.at[side]),
            (fresh.at[2], fresh.at[side]),
            (value_ref, values.at[2 * side]),
        )[kind]
        return halo_copy(kind, src, dst, side)

    def for_sides(kinds, what, sending):
        for side in range(2):
            there = has_above if (side == 0) == sending else has_below

            @pl.when(there)
            def _(side=side):
                for kind in kinds:
                    getattr(halo(side, kind), what)()

    pl.semaphore_wait(barrier, n - 1 + nt - 1)
    for_sides((0, 1), "start", True)

    rows_of_slot = lax.broadcasted_iota(jnp.int32, (slot_count, rows), 1)
    pick = jnp.where(rows_of_slot == stale_col, 1.0, 0.0).astype(jnp.bfloat16)
    held = layer_norm(dot(pick, stream_ref[...]), attn_gain).astype(jnp.bfloat16)
    loads[0].wait()
    fresh[2] = (dot(held, w_key[...]) + key_bias).astype(jnp.bfloat16)
    for_sides((2, 3), "start", True)

    def refresh(cache, stale, new_rows):
        row_ids = lax.broadcasted_iota(jnp.int32, (rows, slot_count), 0)
        spread = jnp.where(row_ids == stale[3:4, :slot_count], 1.0, 0.0)
        hit = jnp.sum(spread, axis=1, keepdims=True) > 0.5
        return jnp.where(
            hit, dot(spread.astype(jnp.bfloat16), new_rows), cache.astype(jnp.float32)
        ).astype(jnp.bfloat16)

    keys[1] = refresh(key_ref[...], index_ref[...], fresh[2])
    refreshed_ref[...] = keys[1]
    values[1] = value_ref[...]
    for side in range(2):

        @pl.when(jnp.logical_not(has_below if side == 0 else has_above))
        def _(side=side):
            keys[2 * side] = jnp.zeros((rows, width), jnp.bfloat16)
            values[2 * side] = jnp.zeros((rows, width), jnp.bfloat16)

        @pl.when(has_below if side == 0 else has_above)
        def _(side=side):
            for kind in range(3):
                halo(side, kind).wait_recv()
            keys[2 * side] = refresh(keys[2 * side], stale_near[side], fresh[side])

    allowed = query_seg == key_seg

    def window(head):
        first = head * head_size // 128 * 128
        last = min(first + 256, width)
        lane = lax.broadcasted_iota(jnp.int32, (rows, last - first), 1) + first
        mine = (lane >= head * head_size) & (lane < (head + 1) * head_size)
        return slice(first, last), mine

    for head in range(HEADS):
        cols, mine = window(head)
        query = jnp.where(mine, query_ref[:, cols].astype(jnp.float32), 0.0).astype(jnp.bfloat16)
        near = keys[:, :, cols].reshape(3 * rows, cols.stop - cols.start)
        scores = lax.dot_general(
            query, near, (((1,), (1,)), ((), ())), preferred_element_type=jnp.float32
        ) * (1.0 / head_size**0.5)
        scores = jnp.where(allowed, scores, -jnp.inf)
        weights = jnp.exp(scores - jnp.max(scores, axis=-1, keepdims=True))
        probs[head] = (weights / jnp.sum(weights, axis=-1, keepdims=True)).astype(jnp.bfloat16)

    for_sides((3,), "wait_recv", False)
    attended[...] = jnp.zeros_like(attended)
    for head in range(HEADS):
        cols, mine = window(head)
        near = values[:, :, cols].reshape(3 * rows, cols.stop - cols.start)
        attended[:, cols] += jnp.where(mine, dot(probs[head], near), 0.0)
    att_ref[...] = attended[...].astype(jnp.bfloat16)
    mixed = stream_ref[...].astype(jnp.float32) + att_ref[...].astype(jnp.float32)
    gath[blk] = layer_norm(mixed, mlp_gain).astype(jnp.bfloat16)

    def passed(block, target, sems):
        return pltpu.make_async_remote_copy(
            src_ref=gath.at[block],
            dst_ref=gath.at[block],
            send_sem=sems.at[block],
            recv_sem=ag_recv.at[block],
            device_id={"blk": target},
            device_id_type=MESH,
        )

    def partial_copy(block):
        return pltpu.make_async_remote_copy(
            src_ref=part.at[block],
            dst_ref=landed.at[blk],
            send_sem=rs_send.at[block],
            recv_sem=rs_recv.at[blk],
            device_id={"blk": block},
            device_id_type=MESH,
        )

    def got(block):
        passed(block, partner, cross_send).wait_recv()

    @pl.when(hi + 1 < line)
    def _():
        passed(blk, blk + 2, up_send).start()

    @pl.when(hi > 0)
    def _():
        passed(blk, blk - 2, down_send).start()

    passed(blk, partner, cross_send).start()
    loads[1].wait()
    loads[2].wait()
    pool = pool_matrix(2 * groups)
    chunk = min(units, 256)

    def work(pair):
        block_rows = gath[pl.ds(2 * pair, 2)].reshape(2 * rows, width)
        for k in range(units // chunk):
            cols = slice(k * chunk, (k + 1) * chunk)
            pre = dot(block_rows, w_fc[:, cols]) + b_fc[:, cols]
            act = (0.5 * pre * (1.0 + lax.erf(pre * 0.7071067811865476))).astype(jnp.bfloat16)
            pooled_units[:, cols] = dot(pool, act).astype(jnp.bfloat16)
        result = dot(pooled_units[...], w_proj[...]).astype(jnp.bfloat16)
        for k in range(2):
            part[2 * pair + k] = result[k * groups : (k + 1) * groups]
        for k in range(2):
            block = 2 * pair + k

            @pl.when(block != blk)
            def _(block=block):
                partial_copy(block).start()

    def step(s, carry):
        below = hi - s
        above = hi + s

        @pl.when((s < line) & (below >= 0))
        def _():
            block = 2 * below + lo
            got(block)

            @pl.when(hi + 1 < line)
            def _():
                passed(block, blk + 2, up_send).start()

            passed(block, partner, cross_send).start()

        @pl.when((s < line) & (above < line))
        def _():
            block = 2 * above + lo
            got(block)

            @pl.when(hi > 0)
            def _():
                passed(block, blk - 2, down_send).start()

            passed(block, partner, cross_send).start()

        def side(d, inner):
            pair = hi + (2 * d - 1) * (s - 1)

            @pl.when((pair >= 0) & (pair < line) & ((d == 0) | (s > 1)))
            def _():
                got(2 * pair + 1 - lo)
                work(pair)

            return inner

        return lax.fori_loop(0, 2, side, carry)

    lax.fori_loop(1, line + 1, step, 0)

    total[...] = part[blk].astype(jnp.float32)

    def collect(k, carry):
        source = lax.rem(blk + k, n)
        pltpu.make_async_remote_copy(
            src_ref=part.at[source],
            dst_ref=landed.at[source],
            send_sem=rs_send.at[source],
            recv_sem=rs_recv.at[source],
            device_id={"blk": source},
            device_id_type=MESH,
        ).wait_recv()
        total[...] += landed[source].astype(jnp.float32)
        return carry

    lax.fori_loop(1, n, collect, 0)
    pool_own = pool_matrix(groups)
    own = dot(pool_own, stream_ref[...]) + dot(pool_own, att_ref[...])
    pooled = (own + total[...]) * 0.25 + b_proj
    merge_in = layer_norm(pooled, merge_gain).astype(jnp.bfloat16)
    loads[3].wait()
    merged = (dot(merge_in, w_merge[...]) + b_merge).astype(jnp.bfloat16)
    first = lax.broadcasted_iota(jnp.int32, (groups, groups), 0)
    second = lax.broadcasted_iota(jnp.int32, (groups, groups), 1)
    same = (owner_col == owner_row) & (first < second)
    ranking = jnp.sum(jnp.where(same, 1.0, 0.0), axis=0, keepdims=True).astype(jnp.int32)
    place = owner_row * groups + ranking
    slots = lax.broadcasted_iota(jnp.int32, (nt * groups, groups), 0)
    selector = jnp.where(slots == place, 1.0, 0.0).astype(jnp.bfloat16)
    outgoing[...] = dot(selector, merged).astype(jnp.bfloat16).reshape(nt, groups, width)

    def delivery(owner, source):
        return pltpu.make_async_remote_copy(
            src_ref=outgoing.at[owner],
            dst_ref=arrived.at[source],
            send_sem=out_send.at[owner],
            recv_sem=out_recv.at[source],
            device_id={"tok": owner},
            device_id_type=MESH,
        )

    for k in range(1, nt):
        delivery(lax.rem(tok + k, nt), tok).start()
    out_ref[tok] = outgoing[tok]

    def settle(j, carry):
        block = 2 * j + lo

        @pl.when((j <= hi) & (hi + 1 < line))
        def _():
            passed(block, blk + 2, up_send).wait_send()

        @pl.when((j >= hi) & (hi > 0))
        def _():
            passed(block, blk - 2, down_send).wait_send()

        passed(block, partner, cross_send).wait_send()
        return carry

    lax.fori_loop(0, line, settle, 0)
    for_sides((0, 1, 2, 3), "wait_send", True)

    def settle_partial(k, carry):
        partial_copy(lax.rem(blk + k, n)).wait_send()
        return carry

    lax.fori_loop(1, n, settle_partial, 0)
    for k in range(1, nt):
        other = lax.rem(tok + k, nt)
        delivery(other, other).wait_recv()
        out_ref[other] = arrived[other]
    for k in range(1, nt):
        delivery(lax.rem(tok + k, nt), tok).wait_send()


def block_kernel(
    stream,
    queries,
    key_cache,
    value_cache,
    index,
    slot_count,
    attn_gain,
    w_key,
    key_bias,
    mlp_gain,
    w_fc,
    b_fc,
    w_proj,
    b_proj,
    merge_gain,
    w_merge,
    b_merge,
):
    n, nt = lax.axis_size("blk"), lax.axis_size("tok")
    rows, width = stream.shape
    groups = rows // 4
    units = w_fc.shape[1]
    vmem = pl.BlockSpec(memory_space=pltpu.VMEM)
    hbm = pl.BlockSpec(memory_space=pl.ANY)
    return pl.pallas_call(
        functools.partial(mlp_kernel, n, nt),
        out_shape=(
            jax.ShapeDtypeStruct((rows, width), jnp.bfloat16),
            jax.ShapeDtypeStruct((nt, groups, width), jnp.bfloat16),
        ),
        in_specs=[vmem] * 12 + [hbm] * 4,
        out_specs=(vmem, vmem),
        scratch_shapes=[
            pltpu.VMEM((3, rows, width), jnp.bfloat16),
            pltpu.VMEM((3, rows, width), jnp.bfloat16),
            pltpu.VMEM((3, slot_count, width), jnp.bfloat16),
            pltpu.VMEM((2, 8, 128), jnp.int32),
            pltpu.VMEM((HEADS, rows, 3 * rows), jnp.bfloat16),
            pltpu.VMEM((rows, width), jnp.float32),
            pltpu.VMEM((rows, width), jnp.bfloat16),
            pltpu.VMEM((n, rows, width), jnp.bfloat16),
            pltpu.VMEM(w_key.shape, jnp.bfloat16),
            pltpu.VMEM(w_fc.shape, jnp.bfloat16),
            pltpu.VMEM(w_proj.shape, jnp.bfloat16),
            pltpu.VMEM(w_merge.shape, jnp.bfloat16),
            pltpu.VMEM((2 * groups, units), jnp.bfloat16),
            pltpu.VMEM((n, groups, width), jnp.bfloat16),
            pltpu.VMEM((n, groups, width), jnp.bfloat16),
            pltpu.VMEM((groups, width), jnp.float32),
            pltpu.VMEM((nt, groups, width), jnp.bfloat16),
            pltpu.VMEM((nt, groups, width), jnp.bfloat16),
            pltpu.SemaphoreType.DMA((4,)),
            pltpu.SemaphoreType.DMA((4, 2)),
            pltpu.SemaphoreType.DMA((4, 2)),
            pltpu.SemaphoreType.DMA((n,)),
            pltpu.SemaphoreType.DMA((n,)),
            pltpu.SemaphoreType.DMA((n,)),
            pltpu.SemaphoreType.DMA((n,)),
            pltpu.SemaphoreType.DMA((n,)),
            pltpu.SemaphoreType.DMA((n,)),
            pltpu.SemaphoreType.DMA((nt,)),
            pltpu.SemaphoreType.DMA((nt,)),
        ],
        compiler_params=pltpu.CompilerParams(
            collective_id=1, has_side_effects=True, vmem_limit_bytes=56 * 1024 * 1024
        ),
    )(
        stream,
        queries,
        key_cache,
        value_cache,
        index,
        attn_gain,
        key_bias,
        mlp_gain,
        b_fc,
        b_proj,
        merge_gain,
        b_merge,
        w_key,
        w_fc,
        w_proj,
        w_merge,
    )


def body(
    stream,
    queries,
    key_cache,
    value_cache,
    segments,
    stale_rows,
    owners,
    attn_gain,
    w_key,
    key_bias,
    mlp_gain,
    w_fc,
    b_fc,
    w_proj,
    b_proj,
    merge_gain,
    w_merge,
    b_merge,
):
    row_count = stream.shape[0]
    model_width = stream.shape[1]
    position = lax.axis_index("blk")
    blocks = lax.axis_size("blk")
    edged = jnp.pad(
        segments.reshape(blocks, row_count), ((1, 1), (0, 0)), constant_values=-1
    )
    segs = lax.dynamic_slice(edged, (position, 0), (3, row_count))
    lanes = -(-row_count // 128) * 128

    def widened(line):
        return jnp.pad(line, ((0, 0), (0, lanes - line.shape[1])), constant_values=-1)

    index = jnp.concatenate(
        [
            widened(segs),
            widened((stale_rows % row_count)[None]),
            widened(owners[None]),
            jnp.full((3, lanes), -1, jnp.int32),
        ],
        axis=0,
    )
    slot_count = -(-stale_rows.shape[0] // 16) * 16
    refreshed, arrived = block_kernel(
        stream,
        queries,
        key_cache,
        value_cache,
        index,
        slot_count,
        attn_gain,
        w_key,
        key_bias,
        mlp_gain,
        w_fc,
        b_fc,
        w_proj,
        b_proj,
        merge_gain,
        w_merge,
        b_merge,
    )
    return (refreshed, arrived.reshape(1, 1, row_count, model_width))


def solution(mesh):
    return jax.shard_map(
        body,
        mesh=mesh,
        in_specs=(
            P(("tok", "blk"), None),
            P(("tok", "blk"), None),
            P(("tok", "blk"), None),
            P(("tok", "blk"), None),
            P("tok"),
            P(("tok", "blk")),
            P(("tok", "blk")),
            P(),
            P(),
            P(),
            P(),
            P(None, "blk"),
            P("blk"),
            P("blk", None),
            P(),
            P(),
            P(),
            P(),
        ),
        out_specs=(P(("tok", "blk"), None), P("tok", "blk", None, None)),
        check_vma=False,
    )
```

```python
import functools

import jax
import jax.numpy as jnp
from jax import lax
from jax.experimental import pallas as pl
from jax.experimental.pallas import tpu as pltpu
from jax.sharding import PartitionSpec as P

HEADS = 16
MESH = pl.DeviceIdType.MESH


def layer_norm(values, gain):
    center = values - jnp.mean(values, axis=-1, keepdims=True)
    spread = jnp.mean(center * center, axis=-1, keepdims=True)
    return center * lax.rsqrt(spread + 1e-06) * gain


def pool_matrix(groups):
    rows = lax.broadcasted_iota(jnp.int32, (groups, groups * 4), 1)
    group = lax.broadcasted_iota(jnp.int32, (groups, groups * 4), 0) * 4
    inside = (rows >= group) & (rows < group + 4)
    return jnp.where(inside, 1.0, 0.0).astype(jnp.bfloat16)


def column(row):
    size = row.shape[1]
    first = lax.broadcasted_iota(jnp.int32, (size, size), 0)
    second = lax.broadcasted_iota(jnp.int32, (size, size), 1)
    spread = jnp.where(first == second, row.astype(jnp.float32), 0.0)
    return jnp.sum(spread, axis=1, keepdims=True).astype(jnp.int32)


def dot(a, b):
    return jnp.dot(a, b, preferred_element_type=jnp.float32)


def mlp_kernel(
    n,
    nt,
    stream_ref,
    query_ref,
    key_ref,
    value_ref,
    index_ref,
    attn_gain_ref,
    key_bias_ref,
    mlp_gain_ref,
    b_fc_ref,
    b_proj_ref,
    merge_gain_ref,
    b_merge_ref,
    w_key_hbm,
    w_fc_hbm,
    w_proj_hbm,
    w_merge_hbm,
    refreshed_ref,
    out_ref,
    keys,
    values,
    fresh,
    stale_near,
    probs,
    attended,
    att_ref,
    gath,
    w_key,
    w_fc,
    w_proj,
    w_merge,
    pooled_units,
    part,
    landed,
    total,
    outgoing,
    arrived,
    weight_sem,
    halo_send,
    halo_recv,
    ag_recv,
    up_send,
    down_send,
    cross_send,
    rs_send,
    rs_recv,
    out_send,
    out_recv,
):
    rows = stream_ref.shape[0]
    groups = rows // 4
    width = stream_ref.shape[1]
    units = b_fc_ref.shape[0]
    line = n // 2
    attn_gain, key_bias, mlp_gain, b_fc, b_proj, merge_gain, b_merge = (
        ref[...].reshape(1, ref.shape[0])
        for ref in (
            attn_gain_ref,
            key_bias_ref,
            mlp_gain_ref,
            b_fc_ref,
            b_proj_ref,
            merge_gain_ref,
            b_merge_ref,
        )
    )
    key_seg = jnp.concatenate([index_ref[k : k + 1, :rows] for k in range(3)], axis=1)
    query_seg = column(index_ref[1:2, :rows])
    slot_count = fresh.shape[1]
    stale_col = column(index_ref[3:4, :slot_count])
    owner_row = index_ref[4:5, :groups]
    owner_col = column(owner_row)
    blk = lax.axis_index("blk")
    tok = lax.axis_index("tok")
    lo = lax.rem(blk, 2)
    hi = lax.div(blk, 2)
    partner = blk + 1 - 2 * lo

    loads = [
        pltpu.make_async_copy(src, dst, weight_sem.at[k])
        for k, (src, dst) in enumerate(
            (
                (w_key_hbm, w_key),
                (w_fc_hbm, w_fc),
                (w_proj_hbm, w_proj),
                (w_merge_hbm, w_merge),
            )
        )
    ]
    for load in loads:
        load.start()

    barrier = pltpu.get_barrier_semaphore()
    for k in range(1, n):
        pl.semaphore_signal(
            barrier, inc=1, device_id={"blk": lax.rem(blk + k, n)}, device_id_type=MESH
        )
    for k in range(1, nt):
        pl.semaphore_signal(
            barrier, inc=1, device_id={"tok": lax.rem(tok + k, nt)}, device_id_type=MESH
        )
    head_size = width // HEADS
    has_below = blk > 0
    has_above = blk + 1 < n

    def halo_copy(kind, src, dst, side):
        target = blk + 1 if side == 0 else blk - 1
        return pltpu.make_async_remote_copy(
            src_ref=src,
            dst_ref=dst,
            send_sem=halo_send.at[kind, side],
            recv_sem=halo_recv.at[kind, side],
            device_id={"blk": target},
            device_id_type=MESH,
        )

    def halo(side, kind):
        src, dst = (
            (key_ref, keys.at[2 * side]),
            (index_ref, stale_near.at[side]),
            (fresh.at[2], fresh.at[side]),
            (value_ref, values.at[2 * side]),
        )[kind]
        return halo_copy(kind, src, dst, side)

    def for_sides(kinds, what, sending):
        for side in range(2):
            there = has_above if (side == 0) == sending else has_below

            @pl.when(there)
            def _(side=side):
                for kind in kinds:
                    getattr(halo(side, kind), what)()

    pl.semaphore_wait(barrier, n - 1 + nt - 1)
    for_sides((0, 1), "start", True)

    rows_of_slot = lax.broadcasted_iota(jnp.int32, (slot_count, rows), 1)
    pick = jnp.where(rows_of_slot == stale_col, 1.0, 0.0).astype(jnp.bfloat16)
    held = layer_norm(dot(pick, stream_ref[...]), attn_gain).astype(jnp.bfloat16)
    loads[0].wait()
    fresh[2] = (dot(held, w_key[...]) + key_bias).astype(jnp.bfloat16)
    for_sides((2, 3), "start", True)

    def refresh(cache, stale, new_rows):
        row_ids = lax.broadcasted_iota(jnp.int32, (rows, slot_count), 0)
        spread = jnp.where(row_ids == stale[3:4, :slot_count], 1.0, 0.0)
        hit = jnp.sum(spread, axis=1, keepdims=True) > 0.5
        return jnp.where(
            hit, dot(spread.astype(jnp.bfloat16), new_rows), cache.astype(jnp.float32)
        ).astype(jnp.bfloat16)

    keys[1] = refresh(key_ref[...], index_ref[...], fresh[2])
    refreshed_ref[...] = keys[1]
    values[1] = value_ref[...]
    for side in range(2):

        @pl.when(jnp.logical_not(has_below if side == 0 else has_above))
        def _(side=side):
            keys[2 * side] = jnp.zeros((rows, width), jnp.bfloat16)
            values[2 * side] = jnp.zeros((rows, width), jnp.bfloat16)

        @pl.when(has_below if side == 0 else has_above)
        def _(side=side):
            for kind in range(3):
                halo(side, kind).wait_recv()
            keys[2 * side] = refresh(keys[2 * side], stale_near[side], fresh[side])

    allowed = query_seg == key_seg

    def window(head):
        first = head * head_size // 128 * 128
        last = min(first + 256, width)
        lane = lax.broadcasted_iota(jnp.int32, (rows, last - first), 1) + first
        mine = (lane >= head * head_size) & (lane < (head + 1) * head_size)
        return slice(first, last), mine

    for head in range(HEADS):
        cols, mine = window(head)
        query = jnp.where(mine, query_ref[:, cols].astype(jnp.float32), 0.0).astype(jnp.bfloat16)
        near = keys[:, :, cols].reshape(3 * rows, cols.stop - cols.start)
        scores = lax.dot_general(
            query, near, (((1,), (1,)), ((), ())), preferred_element_type=jnp.float32
        ) * (1.0 / head_size**0.5)
        scores = jnp.where(allowed, scores, -jnp.inf)
        weights = jnp.exp(scores - jnp.max(scores, axis=-1, keepdims=True))
        probs[head] = (weights / jnp.sum(weights, axis=-1, keepdims=True)).astype(jnp.bfloat16)

    attended[...] = jnp.zeros_like(attended)

    def attend(slot):
        for head in range(HEADS):
            cols, mine = window(head)
            share = probs[head, :, slot * rows : (slot + 1) * rows]
            attended[:, cols] += jnp.where(mine, dot(share, values[slot, :, cols]), 0.0)

    attend(1)
    for side in range(2):

        @pl.when(has_below if side == 0 else has_above)
        def _(side=side):
            halo(side, 3).wait_recv()
            attend(2 * side)

    att_ref[...] = attended[...].astype(jnp.bfloat16)
    mixed = stream_ref[...].astype(jnp.float32) + att_ref[...].astype(jnp.float32)
    gath[blk] = layer_norm(mixed, mlp_gain).astype(jnp.bfloat16)

    def passed(block, target, sems):
        return pltpu.make_async_remote_copy(
            src_ref=gath.at[block],
            dst_ref=gath.at[block],
            send_sem=sems.at[block],
            recv_sem=ag_recv.at[block],
            device_id={"blk": target},
            device_id_type=MESH,
        )

    def partial_copy(block):
        return pltpu.make_async_remote_copy(
            src_ref=part.at[block],
            dst_ref=landed.at[blk],
            send_sem=rs_send.at[block],
            recv_sem=rs_recv.at[blk],
            device_id={"blk": block},
            device_id_type=MESH,
        )

    def got(block):
        passed(block, partner, cross_send).wait_recv()

    @pl.when(hi + 1 < line)
    def _():
        passed(blk, blk + 2, up_send).start()

    @pl.when(hi > 0)
    def _():
        passed(blk, blk - 2, down_send).start()

    passed(blk, partner, cross_send).start()
    loads[1].wait()
    loads[2].wait()
    pool = pool_matrix(groups)
    chunk = min(units, 256)

    def half(pair, side):
        block_rows = gath[2 * pair + side]
        for k in range(units // chunk):
            cols = slice(k * chunk, (k + 1) * chunk)
            pre = dot(block_rows, w_fc[:, cols]) + b_fc[:, cols]
            act = (0.5 * pre * (1.0 + lax.erf(pre * 0.7071067811865476))).astype(jnp.bfloat16)
            pooled_units[side, :, cols] = dot(pool, act).astype(jnp.bfloat16)

    def work(pair):
        half(pair, lo)
        got(2 * pair + 1 - lo)
        half(pair, 1 - lo)
        both = pooled_units[...].reshape(2 * groups, units)
        result = dot(both, w_proj[...]).astype(jnp.bfloat16)
        for k in range(2):
            part[2 * pair + k] = result[k * groups : (k + 1) * groups]
        for k in range(2):
            block = 2 * pair + k

            @pl.when(block != blk)
            def _(block=block):
                partial_copy(block).start()

    def step(s, carry):
        below = hi - s
        above = hi + s

        @pl.when((s < line) & (below >= 0))
        def _():
            block = 2 * below + lo
            got(block)

            @pl.when(hi + 1 < line)
            def _():
                passed(block, blk + 2, up_send).start()

            passed(block, partner, cross_send).start()

        @pl.when((s < line) & (above < line))
        def _():
            block = 2 * above + lo
            got(block)

            @pl.when(hi > 0)
            def _():
                passed(block, blk - 2, down_send).start()

            passed(block, partner, cross_send).start()

        def side(d, inner):
            pair = hi + (2 * d - 1) * (s - 1)

            @pl.when((pair >= 0) & (pair < line) & ((d == 0) | (s > 1)))
            def _():
                work(pair)

            return inner

        return lax.fori_loop(0, 2, side, carry)

    lax.fori_loop(1, line + 1, step, 0)

    total[...] = part[blk].astype(jnp.float32)

    def collect(k, carry):
        source = lax.rem(blk + k, n)
        pltpu.make_async_remote_copy(
            src_ref=part.at[source],
            dst_ref=landed.at[source],
            send_sem=rs_send.at[source],
            recv_sem=rs_recv.at[source],
            device_id={"blk": source},
            device_id_type=MESH,
        ).wait_recv()
        total[...] += landed[source].astype(jnp.float32)
        return carry

    lax.fori_loop(1, n, collect, 0)
    pool_own = pool_matrix(groups)
    own = dot(pool_own, stream_ref[...]) + dot(pool_own, att_ref[...])
    pooled = (own + total[...]) * 0.25 + b_proj
    merge_in = layer_norm(pooled, merge_gain).astype(jnp.bfloat16)
    loads[3].wait()
    merged = (dot(merge_in, w_merge[...]) + b_merge).astype(jnp.bfloat16)
    first = lax.broadcasted_iota(jnp.int32, (groups, groups), 0)
    second = lax.broadcasted_iota(jnp.int32, (groups, groups), 1)
    same = (owner_col == owner_row) & (first < second)
    ranking = jnp.sum(jnp.where(same, 1.0, 0.0), axis=0, keepdims=True).astype(jnp.int32)
    place = owner_row * groups + ranking
    slots = lax.broadcasted_iota(jnp.int32, (nt * groups, groups), 0)
    selector = jnp.where(slots == place, 1.0, 0.0).astype(jnp.bfloat16)
    outgoing[...] = dot(selector, merged).astype(jnp.bfloat16).reshape(nt, groups, width)

    def delivery(owner, source):
        return pltpu.make_async_remote_copy(
            src_ref=outgoing.at[owner],
            dst_ref=arrived.at[source],
            send_sem=out_send.at[owner],
            recv_sem=out_recv.at[source],
            device_id={"tok": owner},
            device_id_type=MESH,
        )

    for k in range(1, nt):
        delivery(lax.rem(tok + k, nt), tok).start()
    out_ref[tok] = outgoing[tok]

    def settle(j, carry):
        block = 2 * j + lo

        @pl.when((j <= hi) & (hi + 1 < line))
        def _():
            passed(block, blk + 2, up_send).wait_send()

        @pl.when((j >= hi) & (hi > 0))
        def _():
            passed(block, blk - 2, down_send).wait_send()

        passed(block, partner, cross_send).wait_send()
        return carry

    lax.fori_loop(0, line, settle, 0)
    for_sides((0, 1, 2, 3), "wait_send", True)

    def settle_partial(k, carry):
        partial_copy(lax.rem(blk + k, n)).wait_send()
        return carry

    lax.fori_loop(1, n, settle_partial, 0)
    for k in range(1, nt):
        other = lax.rem(tok + k, nt)
        delivery(other, other).wait_recv()
        out_ref[other] = arrived[other]
    for k in range(1, nt):
        delivery(lax.rem(tok + k, nt), tok).wait_send()


def block_kernel(
    stream,
    queries,
    key_cache,
    value_cache,
    index,
    slot_count,
    attn_gain,
    w_key,
    key_bias,
    mlp_gain,
    w_fc,
    b_fc,
    w_proj,
    b_proj,
    merge_gain,
    w_merge,
    b_merge,
):
    n, nt = lax.axis_size("blk"), lax.axis_size("tok")
    rows, width = stream.shape
    groups = rows // 4
    units = w_fc.shape[1]
    vmem = pl.BlockSpec(memory_space=pltpu.VMEM)
    hbm = pl.BlockSpec(memory_space=pl.ANY)
    return pl.pallas_call(
        functools.partial(mlp_kernel, n, nt),
        out_shape=(
            jax.ShapeDtypeStruct((rows, width), jnp.bfloat16),
            jax.ShapeDtypeStruct((nt, groups, width), jnp.bfloat16),
        ),
        in_specs=[vmem] * 12 + [hbm] * 4,
        out_specs=(vmem, vmem),
        scratch_shapes=[
            pltpu.VMEM((3, rows, width), jnp.bfloat16),
            pltpu.VMEM((3, rows, width), jnp.bfloat16),
            pltpu.VMEM((3, slot_count, width), jnp.bfloat16),
            pltpu.VMEM((2, 8, 128), jnp.int32),
            pltpu.VMEM((HEADS, rows, 3 * rows), jnp.bfloat16),
            pltpu.VMEM((rows, width), jnp.float32),
            pltpu.VMEM((rows, width), jnp.bfloat16),
            pltpu.VMEM((n, rows, width), jnp.bfloat16),
            pltpu.VMEM(w_key.shape, jnp.bfloat16),
            pltpu.VMEM(w_fc.shape, jnp.bfloat16),
            pltpu.VMEM(w_proj.shape, jnp.bfloat16),
            pltpu.VMEM(w_merge.shape, jnp.bfloat16),
            pltpu.VMEM((2, groups, units), jnp.bfloat16),
            pltpu.VMEM((n, groups, width), jnp.bfloat16),
            pltpu.VMEM((n, groups, width), jnp.bfloat16),
            pltpu.VMEM((groups, width), jnp.float32),
            pltpu.VMEM((nt, groups, width), jnp.bfloat16),
            pltpu.VMEM((nt, groups, width), jnp.bfloat16),
            pltpu.SemaphoreType.DMA((4,)),
            pltpu.SemaphoreType.DMA((4, 2)),
            pltpu.SemaphoreType.DMA((4, 2)),
            pltpu.SemaphoreType.DMA((n,)),
            pltpu.SemaphoreType.DMA((n,)),
            pltpu.SemaphoreType.DMA((n,)),
            pltpu.SemaphoreType.DMA((n,)),
            pltpu.SemaphoreType.DMA((n,)),
            pltpu.SemaphoreType.DMA((n,)),
            pltpu.SemaphoreType.DMA((nt,)),
            pltpu.SemaphoreType.DMA((nt,)),
        ],
        compiler_params=pltpu.CompilerParams(
            collective_id=1, has_side_effects=True, vmem_limit_bytes=56 * 1024 * 1024
        ),
    )(
        stream,
        queries,
        key_cache,
        value_cache,
        index,
        attn_gain,
        key_bias,
        mlp_gain,
        b_fc,
        b_proj,
        merge_gain,
        b_merge,
        w_key,
        w_fc,
        w_proj,
        w_merge,
    )


def body(
    stream,
    queries,
    key_cache,
    value_cache,
    segments,
    stale_rows,
    owners,
    attn_gain,
    w_key,
    key_bias,
    mlp_gain,
    w_fc,
    b_fc,
    w_proj,
    b_proj,
    merge_gain,
    w_merge,
    b_merge,
):
    row_count = stream.shape[0]
    model_width = stream.shape[1]
    position = lax.axis_index("blk")
    blocks = lax.axis_size("blk")
    edged = jnp.pad(
        segments.reshape(blocks, row_count), ((1, 1), (0, 0)), constant_values=-1
    )
    segs = lax.dynamic_slice(edged, (position, 0), (3, row_count))
    lanes = -(-row_count // 128) * 128

    def widened(line):
        return jnp.pad(line, ((0, 0), (0, lanes - line.shape[1])), constant_values=-1)

    index = jnp.concatenate(
        [
            widened(segs),
            widened((stale_rows % row_count)[None]),
            widened(owners[None]),
            jnp.full((3, lanes), -1, jnp.int32),
        ],
        axis=0,
    )
    slot_count = -(-stale_rows.shape[0] // 16) * 16
    refreshed, arrived = block_kernel(
        stream,
        queries,
        key_cache,
        value_cache,
        index,
        slot_count,
        attn_gain,
        w_key,
        key_bias,
        mlp_gain,
        w_fc,
        b_fc,
        w_proj,
        b_proj,
        merge_gain,
        w_merge,
        b_merge,
    )
    return (refreshed, arrived.reshape(1, 1, row_count, model_width))


def solution(mesh):
    return jax.shard_map(
        body,
        mesh=mesh,
        in_specs=(
            P(("tok", "blk"), None),
            P(("tok", "blk"), None),
            P(("tok", "blk"), None),
            P(("tok", "blk"), None),
            P("tok"),
            P(("tok", "blk")),
            P(("tok", "blk")),
            P(),
            P(),
            P(),
            P(),
            P(None, "blk"),
            P("blk"),
            P("blk", None),
            P(),
            P(),
            P(),
            P(),
        ),
        out_specs=(P(("tok", "blk"), None), P("tok", "blk", None, None)),
        check_vma=False,
    )
```

```python
import functools

import jax
import jax.numpy as jnp
from jax import lax
from jax.experimental import pallas as pl
from jax.experimental.pallas import tpu as pltpu
from jax.sharding import PartitionSpec as P

HEADS = 16
MESH = pl.DeviceIdType.MESH


def layer_norm(values, gain):
    center = values - jnp.mean(values, axis=-1, keepdims=True)
    spread = jnp.mean(center * center, axis=-1, keepdims=True)
    return center * lax.rsqrt(spread + 1e-06) * gain


def pool_matrix(groups):
    rows = lax.broadcasted_iota(jnp.int32, (groups, groups * 4), 1)
    group = lax.broadcasted_iota(jnp.int32, (groups, groups * 4), 0) * 4
    inside = (rows >= group) & (rows < group + 4)
    return jnp.where(inside, 1.0, 0.0).astype(jnp.bfloat16)


def column(row):
    size = row.shape[1]
    first = lax.broadcasted_iota(jnp.int32, (size, size), 0)
    second = lax.broadcasted_iota(jnp.int32, (size, size), 1)
    spread = jnp.where(first == second, row.astype(jnp.float32), 0.0)
    return jnp.sum(spread, axis=1, keepdims=True).astype(jnp.int32)


def dot(a, b):
    return jnp.dot(a, b, preferred_element_type=jnp.float32)


def mlp_kernel(
    n,
    nt,
    stream_ref,
    query_ref,
    key_ref,
    value_ref,
    index_ref,
    attn_gain_ref,
    key_bias_ref,
    mlp_gain_ref,
    b_fc_ref,
    b_proj_ref,
    merge_gain_ref,
    b_merge_ref,
    w_key_hbm,
    w_fc_hbm,
    w_proj_hbm,
    w_merge_hbm,
    refreshed_ref,
    out_ref,
    keys,
    values,
    fresh,
    stale_near,
    probs,
    attended,
    att_ref,
    gath,
    w_key,
    w_fc,
    w_proj,
    w_merge,
    pooled_units,
    part,
    landed,
    total,
    side_sum,
    side_sem,
    outgoing,
    arrived,
    weight_sem,
    halo_send,
    halo_recv,
    ag_recv,
    up_send,
    down_send,
    cross_send,
    rs_send,
    rs_recv,
    out_send,
    out_recv,
):
    rows = stream_ref.shape[0]
    groups = rows // 4
    width = stream_ref.shape[1]
    units = b_fc_ref.shape[0]
    line = n // 2
    attn_gain, key_bias, mlp_gain, b_fc, b_proj, merge_gain, b_merge = (
        ref[...].reshape(1, ref.shape[0])
        for ref in (
            attn_gain_ref,
            key_bias_ref,
            mlp_gain_ref,
            b_fc_ref,
            b_proj_ref,
            merge_gain_ref,
            b_merge_ref,
        )
    )
    key_seg = jnp.concatenate([index_ref[k : k + 1, :rows] for k in range(3)], axis=1)
    query_seg = column(index_ref[1:2, :rows])
    slot_count = fresh.shape[1]
    stale_col = column(index_ref[3:4, :slot_count])
    owner_row = index_ref[4:5, :groups]
    owner_col = column(owner_row)
    blk = lax.axis_index("blk")
    tok = lax.axis_index("tok")
    lo = lax.rem(blk, 2)
    hi = lax.div(blk, 2)
    partner = blk + 1 - 2 * lo

    loads = [
        pltpu.make_async_copy(src, dst, weight_sem.at[k])
        for k, (src, dst) in enumerate(
            (
                (w_key_hbm, w_key),
                (w_fc_hbm, w_fc),
                (w_proj_hbm, w_proj),
                (w_merge_hbm, w_merge),
            )
        )
    ]
    for load in loads:
        load.start()

    barrier = pltpu.get_barrier_semaphore()
    for k in range(1, n):
        pl.semaphore_signal(
            barrier, inc=1, device_id={"blk": lax.rem(blk + k, n)}, device_id_type=MESH
        )
    for k in range(1, nt):
        pl.semaphore_signal(
            barrier, inc=1, device_id={"tok": lax.rem(tok + k, nt)}, device_id_type=MESH
        )
    head_size = width // HEADS
    has_below = blk > 0
    has_above = blk + 1 < n

    def halo_copy(kind, src, dst, side):
        target = blk + 1 if side == 0 else blk - 1
        return pltpu.make_async_remote_copy(
            src_ref=src,
            dst_ref=dst,
            send_sem=halo_send.at[kind, side],
            recv_sem=halo_recv.at[kind, side],
            device_id={"blk": target},
            device_id_type=MESH,
        )

    def halo(side, kind):
        src, dst = (
            (key_ref, keys.at[2 * side]),
            (index_ref, stale_near.at[side]),
            (fresh.at[2], fresh.at[side]),
            (value_ref, values.at[2 * side]),
        )[kind]
        return halo_copy(kind, src, dst, side)

    def for_sides(kinds, what, sending):
        for side in range(2):
            there = has_above if (side == 0) == sending else has_below

            @pl.when(there)
            def _(side=side):
                for kind in kinds:
                    getattr(halo(side, kind), what)()

    pl.semaphore_wait(barrier, n - 1 + nt - 1)
    for_sides((0, 1), "start", True)

    rows_of_slot = lax.broadcasted_iota(jnp.int32, (slot_count, rows), 1)
    pick = jnp.where(rows_of_slot == stale_col, 1.0, 0.0).astype(jnp.bfloat16)
    held = layer_norm(dot(pick, stream_ref[...]), attn_gain).astype(jnp.bfloat16)
    loads[0].wait()
    fresh[2] = (dot(held, w_key[...]) + key_bias).astype(jnp.bfloat16)
    for_sides((2, 3), "start", True)

    def refresh(cache, stale, new_rows):
        row_ids = lax.broadcasted_iota(jnp.int32, (rows, slot_count), 0)
        spread = jnp.where(row_ids == stale[3:4, :slot_count], 1.0, 0.0)
        hit = jnp.sum(spread, axis=1, keepdims=True) > 0.5
        return jnp.where(
            hit, dot(spread.astype(jnp.bfloat16), new_rows), cache.astype(jnp.float32)
        ).astype(jnp.bfloat16)

    keys[1] = refresh(key_ref[...], index_ref[...], fresh[2])
    refreshed_ref[...] = keys[1]
    values[1] = value_ref[...]
    for side in range(2):

        @pl.when(jnp.logical_not(has_below if side == 0 else has_above))
        def _(side=side):
            keys[2 * side] = jnp.zeros((rows, width), jnp.bfloat16)
            values[2 * side] = jnp.zeros((rows, width), jnp.bfloat16)

        @pl.when(has_below if side == 0 else has_above)
        def _(side=side):
            for kind in range(3):
                halo(side, kind).wait_recv()
            keys[2 * side] = refresh(keys[2 * side], stale_near[side], fresh[side])

    allowed = query_seg == key_seg

    def window(head):
        first = head * head_size // 128 * 128
        last = min(first + 256, width)
        lane = lax.broadcasted_iota(jnp.int32, (rows, last - first), 1) + first
        mine = (lane >= head * head_size) & (lane < (head + 1) * head_size)
        return slice(first, last), mine

    for head in range(HEADS):
        cols, mine = window(head)
        query = jnp.where(mine, query_ref[:, cols].astype(jnp.float32), 0.0).astype(jnp.bfloat16)
        near = keys[:, :, cols].reshape(3 * rows, cols.stop - cols.start)
        scores = lax.dot_general(
            query, near, (((1,), (1,)), ((), ())), preferred_element_type=jnp.float32
        ) * (1.0 / head_size**0.5)
        scores = jnp.where(allowed, scores, -jnp.inf)
        weights = jnp.exp(scores - jnp.max(scores, axis=-1, keepdims=True))
        probs[head] = (weights / jnp.sum(weights, axis=-1, keepdims=True)).astype(jnp.bfloat16)

    for_sides((3,), "wait_recv", False)
    attended[...] = jnp.zeros_like(attended)
    for head in range(HEADS):
        cols, mine = window(head)
        near = values[:, :, cols].reshape(3 * rows, cols.stop - cols.start)
        attended[:, cols] += jnp.where(mine, dot(probs[head], near), 0.0)
    att_ref[...] = attended[...].astype(jnp.bfloat16)
    mixed = stream_ref[...].astype(jnp.float32) + att_ref[...].astype(jnp.float32)
    gath[blk] = layer_norm(mixed, mlp_gain).astype(jnp.bfloat16)

    def passed(block, target, sems):
        return pltpu.make_async_remote_copy(
            src_ref=gath.at[block],
            dst_ref=gath.at[block],
            send_sem=sems.at[block],
            recv_sem=ag_recv.at[block],
            device_id={"blk": target},
            device_id_type=MESH,
        )

    def partial_copy(pair, source):
        return pltpu.make_async_remote_copy(
            src_ref=part.at[pair],
            dst_ref=landed.at[source],
            send_sem=rs_send.at[pair],
            recv_sem=rs_recv.at[source],
            device_id={"blk": 2 * pair + lo},
            device_id_type=MESH,
        )

    def got(block):
        passed(block, partner, cross_send).wait_recv()

    @pl.when(hi + 1 < line)
    def _():
        passed(blk, blk + 2, up_send).start()

    @pl.when(hi > 0)
    def _():
        passed(blk, blk - 2, down_send).start()

    passed(blk, partner, cross_send).start()
    loads[1].wait()
    loads[2].wait()
    pool = pool_matrix(2 * groups)
    chunk = min(units, 256)

    def work(pair):
        block_rows = gath[pl.ds(2 * pair, 2)].reshape(2 * rows, width)
        for k in range(units // chunk):
            cols = slice(k * chunk, (k + 1) * chunk)
            pre = dot(block_rows, w_fc[:, cols]) + b_fc[:, cols]
            act = (0.5 * pre * (1.0 + lax.erf(pre * 0.7071067811865476))).astype(jnp.bfloat16)
            pooled_units[:, cols] = dot(pool, act).astype(jnp.bfloat16)
        result = dot(pooled_units[...], w_proj[...]).astype(jnp.bfloat16)
        part[pair] = result.reshape(2, groups, width)

        @pl.when(pair != hi)
        def _():
            partial_copy(pair, hi).start()

    def step(s, carry):
        below = hi - s
        above = hi + s

        @pl.when((s < line) & (below >= 0))
        def _():
            block = 2 * below + lo
            got(block)

            @pl.when(hi + 1 < line)
            def _():
                passed(block, blk + 2, up_send).start()

            passed(block, partner, cross_send).start()

        @pl.when((s < line) & (above < line))
        def _():
            block = 2 * above + lo
            got(block)

            @pl.when(hi > 0)
            def _():
                passed(block, blk - 2, down_send).start()

            passed(block, partner, cross_send).start()

        def side(d, inner):
            pair = hi + (2 * d - 1) * (s - 1)

            @pl.when((pair >= 0) & (pair < line) & ((d == 0) | (s > 1)))
            def _():
                got(2 * pair + 1 - lo)
                work(pair)

            return inner

        return lax.fori_loop(0, 2, side, carry)

    lax.fori_loop(1, line + 1, step, 0)

    total[...] = part[hi].astype(jnp.float32)

    def collect(k, carry):
        source = lax.rem(hi + k, line)
        partial_copy(source, source).wait_recv()
        total[...] += landed[source].astype(jnp.float32)
        return carry

    lax.fori_loop(1, line, collect, 0)
    side_sum[0] = total[1 - lo].astype(jnp.bfloat16)
    side_copy = pltpu.make_async_remote_copy(
        src_ref=side_sum.at[0],
        dst_ref=side_sum.at[1],
        send_sem=side_sem.at[0],
        recv_sem=side_sem.at[1],
        device_id={"blk": partner},
        device_id_type=MESH,
    )
    side_copy.start()
    pool_own = pool_matrix(groups)
    own = dot(pool_own, stream_ref[...]) + dot(pool_own, att_ref[...])
    side_copy.wait()
    pooled = (own + total[lo] + side_sum[1].astype(jnp.float32)) * 0.25 + b_proj
    merge_in = layer_norm(pooled, merge_gain).astype(jnp.bfloat16)
    loads[3].wait()
    merged = (dot(merge_in, w_merge[...]) + b_merge).astype(jnp.bfloat16)
    first = lax.broadcasted_iota(jnp.int32, (groups, groups), 0)
    second = lax.broadcasted_iota(jnp.int32, (groups, groups), 1)
    same = (owner_col == owner_row) & (first < second)
    ranking = jnp.sum(jnp.where(same, 1.0, 0.0), axis=0, keepdims=True).astype(jnp.int32)
    place = owner_row * groups + ranking
    slots = lax.broadcasted_iota(jnp.int32, (nt * groups, groups), 0)
    selector = jnp.where(slots == place, 1.0, 0.0).astype(jnp.bfloat16)
    outgoing[...] = dot(selector, merged).astype(jnp.bfloat16).reshape(nt, groups, width)

    def delivery(owner, source):
        return pltpu.make_async_remote_copy(
            src_ref=outgoing.at[owner],
            dst_ref=arrived.at[source],
            send_sem=out_send.at[owner],
            recv_sem=out_recv.at[source],
            device_id={"tok": owner},
            device_id_type=MESH,
        )

    for k in range(1, nt):
        delivery(lax.rem(tok + k, nt), tok).start()
    out_ref[tok] = outgoing[tok]

    def settle(j, carry):
        block = 2 * j + lo

        @pl.when((j <= hi) & (hi + 1 < line))
        def _():
            passed(block, blk + 2, up_send).wait_send()

        @pl.when((j >= hi) & (hi > 0))
        def _():
            passed(block, blk - 2, down_send).wait_send()

        passed(block, partner, cross_send).wait_send()
        return carry

    lax.fori_loop(0, line, settle, 0)
    for_sides((0, 1, 2, 3), "wait_send", True)

    def settle_partial(k, carry):
        partial_copy(lax.rem(hi + k, line), hi).wait_send()
        return carry

    lax.fori_loop(1, line, settle_partial, 0)
    for k in range(1, nt):
        other = lax.rem(tok + k, nt)
        delivery(other, other).wait_recv()
        out_ref[other] = arrived[other]
    for k in range(1, nt):
        delivery(lax.rem(tok + k, nt), tok).wait_send()


def block_kernel(
    stream,
    queries,
    key_cache,
    value_cache,
    index,
    slot_count,
    attn_gain,
    w_key,
    key_bias,
    mlp_gain,
    w_fc,
    b_fc,
    w_proj,
    b_proj,
    merge_gain,
    w_merge,
    b_merge,
):
    n, nt = lax.axis_size("blk"), lax.axis_size("tok")
    rows, width = stream.shape
    groups = rows // 4
    units = w_fc.shape[1]
    vmem = pl.BlockSpec(memory_space=pltpu.VMEM)
    hbm = pl.BlockSpec(memory_space=pl.ANY)
    return pl.pallas_call(
        functools.partial(mlp_kernel, n, nt),
        out_shape=(
            jax.ShapeDtypeStruct((rows, width), jnp.bfloat16),
            jax.ShapeDtypeStruct((nt, groups, width), jnp.bfloat16),
        ),
        in_specs=[vmem] * 12 + [hbm] * 4,
        out_specs=(vmem, vmem),
        scratch_shapes=[
            pltpu.VMEM((3, rows, width), jnp.bfloat16),
            pltpu.VMEM((3, rows, width), jnp.bfloat16),
            pltpu.VMEM((3, slot_count, width), jnp.bfloat16),
            pltpu.VMEM((2, 8, 128), jnp.int32),
            pltpu.VMEM((HEADS, rows, 3 * rows), jnp.bfloat16),
            pltpu.VMEM((rows, width), jnp.float32),
            pltpu.VMEM((rows, width), jnp.bfloat16),
            pltpu.VMEM((n, rows, width), jnp.bfloat16),
            pltpu.VMEM(w_key.shape, jnp.bfloat16),
            pltpu.VMEM(w_fc.shape, jnp.bfloat16),
            pltpu.VMEM(w_proj.shape, jnp.bfloat16),
            pltpu.VMEM(w_merge.shape, jnp.bfloat16),
            pltpu.VMEM((2 * groups, units), jnp.bfloat16),
            pltpu.VMEM((n // 2, 2, groups, width), jnp.bfloat16),
            pltpu.VMEM((n // 2, 2, groups, width), jnp.bfloat16),
            pltpu.VMEM((2, groups, width), jnp.float32),
            pltpu.VMEM((2, groups, width), jnp.bfloat16),
            pltpu.SemaphoreType.DMA((2,)),
            pltpu.VMEM((nt, groups, width), jnp.bfloat16),
            pltpu.VMEM((nt, groups, width), jnp.bfloat16),
            pltpu.SemaphoreType.DMA((4,)),
            pltpu.SemaphoreType.DMA((4, 2)),
            pltpu.SemaphoreType.DMA((4, 2)),
            pltpu.SemaphoreType.DMA((n,)),
            pltpu.SemaphoreType.DMA((n,)),
            pltpu.SemaphoreType.DMA((n,)),
            pltpu.SemaphoreType.DMA((n,)),
            pltpu.SemaphoreType.DMA((n,)),
            pltpu.SemaphoreType.DMA((n,)),
            pltpu.SemaphoreType.DMA((nt,)),
            pltpu.SemaphoreType.DMA((nt,)),
        ],
        compiler_params=pltpu.CompilerParams(
            collective_id=1, has_side_effects=True, vmem_limit_bytes=56 * 1024 * 1024
        ),
    )(
        stream,
        queries,
        key_cache,
        value_cache,
        index,
        attn_gain,
        key_bias,
        mlp_gain,
        b_fc,
        b_proj,
        merge_gain,
        b_merge,
        w_key,
        w_fc,
        w_proj,
        w_merge,
    )


def body(
    stream,
    queries,
    key_cache,
    value_cache,
    segments,
    stale_rows,
    owners,
    attn_gain,
    w_key,
    key_bias,
    mlp_gain,
    w_fc,
    b_fc,
    w_proj,
    b_proj,
    merge_gain,
    w_merge,
    b_merge,
):
    row_count = stream.shape[0]
    model_width = stream.shape[1]
    position = lax.axis_index("blk")
    blocks = lax.axis_size("blk")
    edged = jnp.pad(
        segments.reshape(blocks, row_count), ((1, 1), (0, 0)), constant_values=-1
    )
    segs = lax.dynamic_slice(edged, (position, 0), (3, row_count))
    lanes = -(-row_count // 128) * 128

    def widened(line):
        return jnp.pad(line, ((0, 0), (0, lanes - line.shape[1])), constant_values=-1)

    index = jnp.concatenate(
        [
            widened(segs),
            widened((stale_rows % row_count)[None]),
            widened(owners[None]),
            jnp.full((3, lanes), -1, jnp.int32),
        ],
        axis=0,
    )
    slot_count = -(-stale_rows.shape[0] // 16) * 16
    refreshed, arrived = block_kernel(
        stream,
        queries,
        key_cache,
        value_cache,
        index,
        slot_count,
        attn_gain,
        w_key,
        key_bias,
        mlp_gain,
        w_fc,
        b_fc,
        w_proj,
        b_proj,
        merge_gain,
        w_merge,
        b_merge,
    )
    return (refreshed, arrived.reshape(1, 1, row_count, model_width))


def solution(mesh):
    return jax.shard_map(
        body,
        mesh=mesh,
        in_specs=(
            P(("tok", "blk"), None),
            P(("tok", "blk"), None),
            P(("tok", "blk"), None),
            P(("tok", "blk"), None),
            P("tok"),
            P(("tok", "blk")),
            P(("tok", "blk")),
            P(),
            P(),
            P(),
            P(),
            P(None, "blk"),
            P("blk"),
            P("blk", None),
            P(),
            P(),
            P(),
            P(),
        ),
        out_specs=(P(("tok", "blk"), None), P("tok", "blk", None, None)),
        check_vma=False,
    )
```

```python
import functools

import jax
import jax.numpy as jnp
from jax import lax
from jax.experimental import pallas as pl
from jax.experimental.pallas import tpu as pltpu
from jax.sharding import PartitionSpec as P

HEADS = 16
MESH = pl.DeviceIdType.MESH


def layer_norm(values, gain):
    center = values - jnp.mean(values, axis=-1, keepdims=True)
    spread = jnp.mean(center * center, axis=-1, keepdims=True)
    return center * lax.rsqrt(spread + 1e-06) * gain


def pool_matrix(groups):
    rows = lax.broadcasted_iota(jnp.int32, (groups, groups * 4), 1)
    group = lax.broadcasted_iota(jnp.int32, (groups, groups * 4), 0) * 4
    inside = (rows >= group) & (rows < group + 4)
    return jnp.where(inside, 1.0, 0.0).astype(jnp.bfloat16)


def column(row):
    size = row.shape[1]
    first = lax.broadcasted_iota(jnp.int32, (size, size), 0)
    second = lax.broadcasted_iota(jnp.int32, (size, size), 1)
    spread = jnp.where(first == second, row.astype(jnp.float32), 0.0)
    return jnp.sum(spread, axis=1, keepdims=True).astype(jnp.int32)


def dot(a, b):
    return jnp.dot(a, b, preferred_element_type=jnp.float32)


def mlp_kernel(
    n,
    nt,
    stream_ref,
    query_ref,
    key_ref,
    value_ref,
    index_ref,
    attn_gain_ref,
    key_bias_ref,
    mlp_gain_ref,
    b_fc_ref,
    b_proj_ref,
    merge_gain_ref,
    b_merge_ref,
    w_key_hbm,
    w_fc_hbm,
    w_proj_hbm,
    w_merge_hbm,
    refreshed_ref,
    out_ref,
    keys,
    values,
    fresh,
    stale_near,
    probs,
    attended,
    att_ref,
    gath,
    w_key,
    w_fc,
    w_proj,
    w_merge,
    pooled_units,
    part,
    landed,
    total,
    side_sum,
    side_sem,
    outgoing,
    arrived,
    weight_sem,
    halo_send,
    halo_recv,
    ag_recv,
    up_send,
    down_send,
    cross_send,
    rs_send,
    rs_recv,
    out_send,
    out_recv,
):
    rows = stream_ref.shape[0]
    groups = rows // 4
    width = stream_ref.shape[1]
    units = b_fc_ref.shape[0]
    line = n // 2
    attn_gain, key_bias, mlp_gain, b_fc, b_proj, merge_gain, b_merge = (
        ref[...].reshape(1, ref.shape[0])
        for ref in (
            attn_gain_ref,
            key_bias_ref,
            mlp_gain_ref,
            b_fc_ref,
            b_proj_ref,
            merge_gain_ref,
            b_merge_ref,
        )
    )
    key_seg = jnp.concatenate([index_ref[k : k + 1, :rows] for k in range(3)], axis=1)
    query_seg = column(index_ref[1:2, :rows])
    slot_count = fresh.shape[1]
    stale_col = column(index_ref[3:4, :slot_count])
    owner_row = index_ref[4:5, :groups]
    owner_col = column(owner_row)
    blk = lax.axis_index("blk")
    tok = lax.axis_index("tok")
    lo = lax.rem(blk, 2)
    hi = lax.div(blk, 2)
    partner = blk + 1 - 2 * lo

    loads = [
        pltpu.make_async_copy(src, dst, weight_sem.at[k])
        for k, (src, dst) in enumerate(
            (
                (w_key_hbm, w_key),
                (w_fc_hbm, w_fc),
                (w_proj_hbm, w_proj),
                (w_merge_hbm, w_merge),
            )
        )
    ]
    for load in loads:
        load.start()

    barrier = pltpu.get_barrier_semaphore()
    for k in range(1, n):
        pl.semaphore_signal(
            barrier, inc=1, device_id={"blk": lax.rem(blk + k, n)}, device_id_type=MESH
        )
    for k in range(1, nt):
        pl.semaphore_signal(
            barrier, inc=1, device_id={"tok": lax.rem(tok + k, nt)}, device_id_type=MESH
        )
    head_size = width // HEADS
    has_below = blk > 0
    has_above = blk + 1 < n

    def halo_copy(kind, src, dst, side):
        target = blk + 1 if side == 0 else blk - 1
        return pltpu.make_async_remote_copy(
            src_ref=src,
            dst_ref=dst,
            send_sem=halo_send.at[kind, side],
            recv_sem=halo_recv.at[kind, side],
            device_id={"blk": target},
            device_id_type=MESH,
        )

    def halo(side, kind):
        src, dst = (
            (key_ref, keys.at[2 * side]),
            (index_ref, stale_near.at[side]),
            (fresh.at[2], fresh.at[side]),
            (value_ref, values.at[2 * side]),
        )[kind]
        return halo_copy(kind, src, dst, side)

    def for_sides(kinds, what, sending):
        for side in range(2):
            there = has_above if (side == 0) == sending else has_below

            @pl.when(there)
            def _(side=side):
                for kind in kinds:
                    getattr(halo(side, kind), what)()

    pl.semaphore_wait(barrier, n - 1 + nt - 1)
    for_sides((0, 1), "start", True)

    rows_of_slot = lax.broadcasted_iota(jnp.int32, (slot_count, rows), 1)
    pick = jnp.where(rows_of_slot == stale_col, 1.0, 0.0).astype(jnp.bfloat16)
    held = layer_norm(dot(pick, stream_ref[...]), attn_gain).astype(jnp.bfloat16)
    loads[0].wait()
    fresh[2] = (dot(held, w_key[...]) + key_bias).astype(jnp.bfloat16)
    for_sides((2, 3), "start", True)

    def refresh(cache, stale, new_rows):
        row_ids = lax.broadcasted_iota(jnp.int32, (rows, slot_count), 0)
        spread = jnp.where(row_ids == stale[3:4, :slot_count], 1.0, 0.0)
        hit = jnp.sum(spread, axis=1, keepdims=True) > 0.5
        return jnp.where(
            hit, dot(spread.astype(jnp.bfloat16), new_rows), cache.astype(jnp.float32)
        ).astype(jnp.bfloat16)

    keys[1] = refresh(key_ref[...], index_ref[...], fresh[2])
    refreshed_ref[...] = keys[1]
    values[1] = value_ref[...]
    for side in range(2):

        @pl.when(jnp.logical_not(has_below if side == 0 else has_above))
        def _(side=side):
            keys[2 * side] = jnp.zeros((rows, width), jnp.bfloat16)
            values[2 * side] = jnp.zeros((rows, width), jnp.bfloat16)

        @pl.when(has_below if side == 0 else has_above)
        def _(side=side):
            for kind in range(3):
                halo(side, kind).wait_recv()
            keys[2 * side] = refresh(keys[2 * side], stale_near[side], fresh[side])

    allowed = query_seg == key_seg

    def window(head):
        first = head * head_size // 128 * 128
        last = min(first + 256, width)
        lane = lax.broadcasted_iota(jnp.int32, (rows, last - first), 1) + first
        mine = (lane >= head * head_size) & (lane < (head + 1) * head_size)
        return slice(first, last), mine

    for head in range(HEADS):
        cols, mine = window(head)
        query = jnp.where(mine, query_ref[:, cols].astype(jnp.float32), 0.0).astype(jnp.bfloat16)
        near = keys[:, :, cols].reshape(3 * rows, cols.stop - cols.start)
        scores = lax.dot_general(
            query, near, (((1,), (1,)), ((), ())), preferred_element_type=jnp.float32
        ) * (1.0 / head_size**0.5)
        scores = jnp.where(allowed, scores, -jnp.inf)
        weights = jnp.exp(scores - jnp.max(scores, axis=-1, keepdims=True))
        probs[head] = (weights / jnp.sum(weights, axis=-1, keepdims=True)).astype(jnp.bfloat16)

    attended[...] = jnp.zeros_like(attended)

    def attend(slot):
        for head in range(HEADS):
            cols, mine = window(head)
            share = probs[head, :, slot * rows : (slot + 1) * rows]
            attended[:, cols] += jnp.where(mine, dot(share, values[slot, :, cols]), 0.0)

    attend(1)
    for side in range(2):

        @pl.when(has_below if side == 0 else has_above)
        def _(side=side):
            halo(side, 3).wait_recv()
            attend(2 * side)

    att_ref[...] = attended[...].astype(jnp.bfloat16)
    mixed = stream_ref[...].astype(jnp.float32) + att_ref[...].astype(jnp.float32)
    gath[blk] = layer_norm(mixed, mlp_gain).astype(jnp.bfloat16)

    def passed(block, target, sems):
        return pltpu.make_async_remote_copy(
            src_ref=gath.at[block],
            dst_ref=gath.at[block],
            send_sem=sems.at[block],
            recv_sem=ag_recv.at[block],
            device_id={"blk": target},
            device_id_type=MESH,
        )

    def partial_copy(pair, source):
        return pltpu.make_async_remote_copy(
            src_ref=part.at[pair],
            dst_ref=landed.at[source],
            send_sem=rs_send.at[pair],
            recv_sem=rs_recv.at[source],
            device_id={"blk": 2 * pair + lo},
            device_id_type=MESH,
        )

    def got(block):
        passed(block, partner, cross_send).wait_recv()

    @pl.when(hi + 1 < line)
    def _():
        passed(blk, blk + 2, up_send).start()

    @pl.when(hi > 0)
    def _():
        passed(blk, blk - 2, down_send).start()

    passed(blk, partner, cross_send).start()
    loads[1].wait()
    loads[2].wait()
    pool = pool_matrix(2 * groups)
    chunk = min(units, 256)

    def work(pair):
        block_rows = gath[pl.ds(2 * pair, 2)].reshape(2 * rows, width)
        for k in range(units // chunk):
            cols = slice(k * chunk, (k + 1) * chunk)
            pre = dot(block_rows, w_fc[:, cols]) + b_fc[:, cols]
            act = (0.5 * pre * (1.0 + lax.erf(pre * 0.7071067811865476))).astype(jnp.bfloat16)
            pooled_units[:, cols] = dot(pool, act).astype(jnp.bfloat16)
        result = dot(pooled_units[...], w_proj[...]).astype(jnp.bfloat16)
        part[pair] = result.reshape(2, groups, width)

        @pl.when(pair != hi)
        def _():
            partial_copy(pair, hi).start()

    def step(s, carry):
        below = hi - s
        above = hi + s

        @pl.when((s < line) & (below >= 0))
        def _():
            block = 2 * below + lo
            got(block)

            @pl.when(hi + 1 < line)
            def _():
                passed(block, blk + 2, up_send).start()

            passed(block, partner, cross_send).start()

        @pl.when((s < line) & (above < line))
        def _():
            block = 2 * above + lo
            got(block)

            @pl.when(hi > 0)
            def _():
                passed(block, blk - 2, down_send).start()

            passed(block, partner, cross_send).start()

        def side(d, inner):
            pair = hi + (2 * d - 1) * (s - 1)

            @pl.when((pair >= 0) & (pair < line) & ((d == 0) | (s > 1)))
            def _():
                got(2 * pair + 1 - lo)
                work(pair)

            return inner

        return lax.fori_loop(0, 2, side, carry)

    lax.fori_loop(1, line + 1, step, 0)

    total[...] = part[hi].astype(jnp.float32)

    def collect(k, carry):
        source = lax.rem(hi + k, line)
        partial_copy(source, source).wait_recv()
        total[...] += landed[source].astype(jnp.float32)
        return carry

    lax.fori_loop(1, line, collect, 0)
    side_sum[0] = total[1 - lo].astype(jnp.bfloat16)
    side_copy = pltpu.make_async_remote_copy(
        src_ref=side_sum.at[0],
        dst_ref=side_sum.at[1],
        send_sem=side_sem.at[0],
        recv_sem=side_sem.at[1],
        device_id={"blk": partner},
        device_id_type=MESH,
    )
    side_copy.start()
    pool_own = pool_matrix(groups)
    own = dot(pool_own, stream_ref[...]) + dot(pool_own, att_ref[...])
    side_copy.wait()
    pooled = (own + total[lo] + side_sum[1].astype(jnp.float32)) * 0.25 + b_proj
    merge_in = layer_norm(pooled, merge_gain).astype(jnp.bfloat16)
    loads[3].wait()
    merged = (dot(merge_in, w_merge[...]) + b_merge).astype(jnp.bfloat16)
    first = lax.broadcasted_iota(jnp.int32, (groups, groups), 0)
    second = lax.broadcasted_iota(jnp.int32, (groups, groups), 1)
    same = (owner_col == owner_row) & (first < second)
    ranking = jnp.sum(jnp.where(same, 1.0, 0.0), axis=0, keepdims=True).astype(jnp.int32)
    place = owner_row * groups + ranking
    slots = lax.broadcasted_iota(jnp.int32, (nt * groups, groups), 0)
    selector = jnp.where(slots == place, 1.0, 0.0).astype(jnp.bfloat16)
    outgoing[...] = dot(selector, merged).astype(jnp.bfloat16).reshape(nt, groups, width)

    def delivery(owner, source):
        return pltpu.make_async_remote_copy(
            src_ref=outgoing.at[owner],
            dst_ref=arrived.at[source],
            send_sem=out_send.at[owner],
            recv_sem=out_recv.at[source],
            device_id={"tok": owner},
            device_id_type=MESH,
        )

    for k in range(1, nt):
        delivery(lax.rem(tok + k, nt), tok).start()
    out_ref[tok] = outgoing[tok]

    def settle(j, carry):
        block = 2 * j + lo

        @pl.when((j <= hi) & (hi + 1 < line))
        def _():
            passed(block, blk + 2, up_send).wait_send()

        @pl.when((j >= hi) & (hi > 0))
        def _():
            passed(block, blk - 2, down_send).wait_send()

        passed(block, partner, cross_send).wait_send()
        return carry

    lax.fori_loop(0, line, settle, 0)
    for_sides((0, 1, 2, 3), "wait_send", True)

    def settle_partial(k, carry):
        partial_copy(lax.rem(hi + k, line), hi).wait_send()
        return carry

    lax.fori_loop(1, line, settle_partial, 0)
    for k in range(1, nt):
        other = lax.rem(tok + k, nt)
        delivery(other, other).wait_recv()
        out_ref[other] = arrived[other]
    for k in range(1, nt):
        delivery(lax.rem(tok + k, nt), tok).wait_send()


def block_kernel(
    stream,
    queries,
    key_cache,
    value_cache,
    index,
    slot_count,
    attn_gain,
    w_key,
    key_bias,
    mlp_gain,
    w_fc,
    b_fc,
    w_proj,
    b_proj,
    merge_gain,
    w_merge,
    b_merge,
):
    n, nt = lax.axis_size("blk"), lax.axis_size("tok")
    rows, width = stream.shape
    groups = rows // 4
    units = w_fc.shape[1]
    vmem = pl.BlockSpec(memory_space=pltpu.VMEM)
    hbm = pl.BlockSpec(memory_space=pl.ANY)
    return pl.pallas_call(
        functools.partial(mlp_kernel, n, nt),
        out_shape=(
            jax.ShapeDtypeStruct((rows, width), jnp.bfloat16),
            jax.ShapeDtypeStruct((nt, groups, width), jnp.bfloat16),
        ),
        in_specs=[vmem] * 12 + [hbm] * 4,
        out_specs=(vmem, vmem),
        scratch_shapes=[
            pltpu.VMEM((3, rows, width), jnp.bfloat16),
            pltpu.VMEM((3, rows, width), jnp.bfloat16),
            pltpu.VMEM((3, slot_count, width), jnp.bfloat16),
            pltpu.VMEM((2, 8, 128), jnp.int32),
            pltpu.VMEM((HEADS, rows, 3 * rows), jnp.bfloat16),
            pltpu.VMEM((rows, width), jnp.float32),
            pltpu.VMEM((rows, width), jnp.bfloat16),
            pltpu.VMEM((n, rows, width), jnp.bfloat16),
            pltpu.VMEM(w_key.shape, jnp.bfloat16),
            pltpu.VMEM(w_fc.shape, jnp.bfloat16),
            pltpu.VMEM(w_proj.shape, jnp.bfloat16),
            pltpu.VMEM(w_merge.shape, jnp.bfloat16),
            pltpu.VMEM((2 * groups, units), jnp.bfloat16),
            pltpu.VMEM((n // 2, 2, groups, width), jnp.bfloat16),
            pltpu.VMEM((n // 2, 2, groups, width), jnp.bfloat16),
            pltpu.VMEM((2, groups, width), jnp.float32),
            pltpu.VMEM((2, groups, width), jnp.bfloat16),
            pltpu.SemaphoreType.DMA((2,)),
            pltpu.VMEM((nt, groups, width), jnp.bfloat16),
            pltpu.VMEM((nt, groups, width), jnp.bfloat16),
            pltpu.SemaphoreType.DMA((4,)),
            pltpu.SemaphoreType.DMA((4, 2)),
            pltpu.SemaphoreType.DMA((4, 2)),
            pltpu.SemaphoreType.DMA((n,)),
            pltpu.SemaphoreType.DMA((n,)),
            pltpu.SemaphoreType.DMA((n,)),
            pltpu.SemaphoreType.DMA((n,)),
            pltpu.SemaphoreType.DMA((n,)),
            pltpu.SemaphoreType.DMA((n,)),
            pltpu.SemaphoreType.DMA((nt,)),
            pltpu.SemaphoreType.DMA((nt,)),
        ],
        compiler_params=pltpu.CompilerParams(
            collective_id=1, has_side_effects=True, vmem_limit_bytes=56 * 1024 * 1024
        ),
    )(
        stream,
        queries,
        key_cache,
        value_cache,
        index,
        attn_gain,
        key_bias,
        mlp_gain,
        b_fc,
        b_proj,
        merge_gain,
        b_merge,
        w_key,
        w_fc,
        w_proj,
        w_merge,
    )


def body(
    stream,
    queries,
    key_cache,
    value_cache,
    segments,
    stale_rows,
    owners,
    attn_gain,
    w_key,
    key_bias,
    mlp_gain,
    w_fc,
    b_fc,
    w_proj,
    b_proj,
    merge_gain,
    w_merge,
    b_merge,
):
    row_count = stream.shape[0]
    model_width = stream.shape[1]
    position = lax.axis_index("blk")
    blocks = lax.axis_size("blk")
    edged = jnp.pad(
        segments.reshape(blocks, row_count), ((1, 1), (0, 0)), constant_values=-1
    )
    segs = lax.dynamic_slice(edged, (position, 0), (3, row_count))
    lanes = -(-row_count // 128) * 128

    def widened(line):
        return jnp.pad(line, ((0, 0), (0, lanes - line.shape[1])), constant_values=-1)

    index = jnp.concatenate(
        [
            widened(segs),
            widened((stale_rows % row_count)[None]),
            widened(owners[None]),
            jnp.full((3, lanes), -1, jnp.int32),
        ],
        axis=0,
    )
    slot_count = -(-stale_rows.shape[0] // 16) * 16
    refreshed, arrived = block_kernel(
        stream,
        queries,
        key_cache,
        value_cache,
        index,
        slot_count,
        attn_gain,
        w_key,
        key_bias,
        mlp_gain,
        w_fc,
        b_fc,
        w_proj,
        b_proj,
        merge_gain,
        w_merge,
        b_merge,
    )
    return (refreshed, arrived.reshape(1, 1, row_count, model_width))


def solution(mesh):
    return jax.shard_map(
        body,
        mesh=mesh,
        in_specs=(
            P(("tok", "blk"), None),
            P(("tok", "blk"), None),
            P(("tok", "blk"), None),
            P(("tok", "blk"), None),
            P("tok"),
            P(("tok", "blk")),
            P(("tok", "blk")),
            P(),
            P(),
            P(),
            P(),
            P(None, "blk"),
            P("blk"),
            P("blk", None),
            P(),
            P(),
            P(),
            P(),
        ),
        out_specs=(P(("tok", "blk"), None), P("tok", "blk", None, None)),
        check_vma=False,
    )
```
